32 devices in a mesh: depth: 8 (over y, x, core), tile: 4 (over z).
Axes of the slice: x: 2, y: 2, z: 4, core: 2. Of those that a mesh axis runs over, the one named last changes fastest.
Arguments:
- coarse: bfloat16 [16, 32, 256], P('depth', None, 'tile'), may hold values from -6 to 6
- residual: bfloat16 [32, 64, 512], P('depth', None, 'tile'), may hold values from -6 to 6
- levels: int32 [8, 16, 128], P('depth', None, 'tile'), may hold values from 0 to 2
- slab_rank: int32 [8], replicated, may hold values from -8 to 7, as said below
- light_angles: float32 [2], replicated, may hold values from -3.140625 to 3.140625
- color_slope: float32 [3], replicated, may hold values from 0.5 to 2
- color_shift: float32 [3], replicated, may hold values from -1 to 1
Outputs:
- image: float32 [4, 64, 512], P(None, 'depth', 'tile')
- slab_shade: float32 [8, 64, 512], P('depth', None, 'tile')
The draws below stay inside these ranges and needn't reach their ends.
Inputs may be any that keep to these rules, and one draw needn't show every extreme that they name: With p = s for every slab s, or p = 7 - s for every slab s, and one whole number c of 1 to 4: slab_rank is p where p >= c and p - 8 where p < c.
All inputs are finite; a program needn't handle non-finite values.
Results may differ from the reference program's by a relative error of at most 0.00079.
Values may be sent and summed in bfloat16 or wider, within the bound.
A program may use at most 192 MiB of HBM per device.

```python
import jax
import jax.numpy as jnp
from jax import lax

DEP = 4
BRICK = 4
NZ = 32
ROWS = 64
COLS = 512


def draw_slab_rank(key, part):
    slabs = NZ // DEP
    flag = jax.random.randint(jax.random.fold_in(key, 17), (), 0, 2)
    offset = jax.random.randint(jax.random.fold_in(key, 29), (), 1, slabs // 2 + 1)
    counted = jnp.arange(slabs, dtype=jnp.int32)
    position = jnp.where(flag == 1, counted, slabs - 1 - counted)
    ranks = jnp.where(position >= offset, position, position - slabs)
    return ranks.astype(jnp.int32)


def touch_ends(drawn, key, least, top_value):
    extent = drawn.shape
    place = [jax.random.randint(jax.random.fold_in(key, axis), (), 0, extent[axis]) for axis in range(len(extent))]
    drawn = drawn.at[tuple(place)].set(least)
    longest = extent.index(max(extent))
    place[longest] = (place[longest] + 1) % extent[longest]
    return drawn.at[tuple(place)].set(top_value)


def block_levels(stream_key, extent, shards, low, high):
    level, own = 1.0, jax.random.fold_in(stream_key, 6)
    for dim, parts in shards:
        steps = jnp.exp(jax.random.uniform(jax.random.fold_in(own, dim), (parts,), jnp.float32, low / len(shards), high / len(shards)))
        level = level * jnp.repeat(steps, extent[dim] // parts).reshape([-1 if axis == dim else 1 for axis in range(len(extent))])
    return level


def centred(stream_key, shape, deviation, most, cuts=(), kind=jnp.bfloat16):
    result = deviation * jax.random.normal(stream_key, shape, jnp.float32)
    if cuts:
        result = result * block_levels(stream_key, shape, cuts, -0.22, 0.18)
    return jnp.clip(result, -most, most).astype(kind)


def setup_inputs(seed: int = 0) -> dict:
    key_list = jax.random.split(jax.random.key(seed), 8)
    coarse = centred(key_list[0], (NZ // 2, ROWS // 2, COLS // 2), 1.0, 6.0, ((0, 8), (2, 4)))
    residual = centred(key_list[1], (NZ, ROWS, COLS), 1.0, 6.0, ((0, 8), (2, 4)))
    levels = touch_ends(jax.random.randint(key_list[2], (NZ // BRICK, ROWS // BRICK, COLS // BRICK), 0, 3), jax.random.fold_in(key_list[2], 1), 0, 2).astype(jnp.int32)
    slab_rank = draw_slab_rank(jax.random.fold_in(key_list[7], 71), 0)
    light_angles = jnp.clip(jax.random.uniform(key_list[4], (2,), jnp.float32, -3.140625, 3.140625), -3.140625, 3.140625)
    color_slope = jnp.clip(jax.random.uniform(key_list[5], (3,), jnp.float32, 0.5, 2.0), 0.5, 2.0)
    color_shift = jnp.clip(jax.random.uniform(key_list[6], (3,), jnp.float32, -1.0, 1.0), -1.0, 1.0)
    return dict(coarse=coarse, residual=residual, levels=levels, slab_rank=slab_rank, light_angles=light_angles, color_slope=color_slope, color_shift=color_shift)


def refine_block(coarse_part, residual_part, level_part):
    dep, rows, cols = residual_part.shape
    lifted = coarse_part.astype(jnp.float32)[:, None, :, None, :, None]
    lifted = jnp.broadcast_to(lifted, (dep // 2, 2, rows // 2, 2, cols // 2, 2)).reshape(dep, rows, cols)
    nb = level_part.shape
    scaled = level_part.astype(jnp.float32)[:, None, :, None, :, None]
    scaled = jnp.broadcast_to(scaled, (nb[0], dep // nb[0], nb[1], rows // nb[1], nb[2], cols // nb[2])).reshape(dep, rows, cols)
    return (lifted + 0.5 * scaled * residual_part.astype(jnp.float32)).astype(jnp.bfloat16)

def light_vector(angles):
    return jnp.stack([jnp.sin(angles[1]), jnp.cos(angles[1]) * jnp.sin(angles[0]), jnp.cos(angles[1]) * jnp.cos(angles[0])])

def render_slab(padded, ascending, step, light, slope, shift):
    f = padded.astype(jnp.float32)
    v = f[2:-2, 2:-2, 2:-2]
    grad_z = (f[:-4, 2:-2, 2:-2] - 8.0 * f[1:-3, 2:-2, 2:-2] + 8.0 * f[3:-1, 2:-2, 2:-2] - f[4:, 2:-2, 2:-2]) / 12.0
    grad_y = (f[2:-2, :-4, 2:-2] - 8.0 * f[2:-2, 1:-3, 2:-2] + 8.0 * f[2:-2, 3:-1, 2:-2] - f[2:-2, 4:, 2:-2]) / 12.0
    grad_x = (f[2:-2, 2:-2, :-4] - 8.0 * f[2:-2, 2:-2, 1:-3] + 8.0 * f[2:-2, 2:-2, 3:-1] - f[2:-2, 2:-2, 4:]) / 12.0
    along = light[0] * grad_z + light[1] * grad_y + light[2] * grad_x
    shade = 0.25 + 0.75 * jnp.abs(along) / jnp.sqrt(grad_z * grad_z + grad_y * grad_y + grad_x * grad_x + 1.0)
    extinct = 4.0 * jax.nn.sigmoid(3.0 * (v - 1.5))
    running = jnp.cumsum(extinct, axis=0)
    total = running[-1]
    before = jnp.where(ascending, running - extinct, total - running)
    weight = jnp.exp(-step * before) * (1.0 - jnp.exp(-step * extinct)) * shade
    colors = [lax.optimization_barrier(jnp.sum(weight * jax.nn.sigmoid(slope[k] * v + shift[k]), axis=0)) for k in range(3)]
    return (jnp.stack(colors + [1.0 - jnp.exp(-step * total)]), lax.optimization_barrier(jnp.mean(shade, axis=0)))

def reference(coarse, residual, levels, slab_rank, light_angles, color_slope, color_shift):
    slabs = NZ // DEP

    def refine(s):
        c = lax.dynamic_slice_in_dim(coarse, s * (DEP // 2), DEP // 2, 0)
        r = lax.dynamic_slice_in_dim(residual, s * DEP, DEP, 0)
        l = lax.dynamic_slice_in_dim(levels, s * (DEP // BRICK), DEP // BRICK, 0)
        return refine_block(c, r, l)
    refined = lax.map(refine, jnp.arange(slabs, dtype=jnp.int32)).reshape(NZ, ROWS, COLS)
    padded = jnp.pad(refined, 2)
    ascending = slab_rank[0] < slab_rank[slabs - 1]
    order = jnp.argsort(slab_rank).astype(jnp.int32)
    light = light_vector(light_angles)
    step = 4.0 / NZ

    def composite(carry, k):
        total, through = carry
        s = order[k]
        piece = lax.dynamic_slice_in_dim(padded, (s * DEP).astype(jnp.int32), DEP + 4, 0)
        slab_image, mean_shade = render_slab(piece, ascending, step, light, color_slope, color_shift)
        visible = (slab_rank[s] >= 0).astype(jnp.float32)
        slab_image = slab_image * visible
        total = total + through[None] * slab_image
        through = through * (1.0 - slab_image[3])
        return ((total, through), mean_shade)
    start = (jnp.zeros((4, ROWS, COLS), jnp.float32), jnp.ones((ROWS, COLS), jnp.float32))
    (image, _), shades = lax.scan(composite, start, jnp.arange(slabs, dtype=jnp.int32))
    slab_shade = jnp.zeros((slabs, ROWS, COLS), jnp.float32).at[order].set(shades)
    return (image, slab_shade)
```

```python
import functools

import jax
import jax.numpy as jnp
from jax import lax
from jax.experimental import pallas as pl
from jax.experimental.pallas import tpu as pltpu
from jax.sharding import PartitionSpec as P

SUB = 8
HALO = 2


def each(count, body):
    if count == 1:
        body(0)
    else:
        lax.fori_loop(0, count, lambda i, _: (body(i), 0)[1], 0)


def repeat_matrix(shape, dim):
    factor = shape[dim] // shape[1 - dim]
    long = lax.broadcasted_iota(jnp.int32, shape, dim)
    short = lax.broadcasted_iota(jnp.int32, shape, 1 - dim) * factor
    return ((long >= short) & (long < short + factor)).astype(jnp.float32).astype(jnp.bfloat16)


def stencil_matrix(cols):
    apart = lax.broadcasted_iota(jnp.int32, (cols, cols), 0) - lax.broadcasted_iota(
        jnp.int32, (cols, cols), 1
    )
    value = jnp.where(apart == -2, 1.0, 0.0)
    value = jnp.where(apart == -1, -8.0, value)
    value = jnp.where(apart == 1, 8.0, value)
    value = jnp.where(apart == 2, -1.0, value)
    return value.astype(jnp.bfloat16)


def matmul(a, b):
    return jnp.dot(a, b, preferred_element_type=jnp.float32)


def kernel(
    slabs,
    tiles,
    coarse_in,
    residual_in,
    levels_in,
    rank_in,
    angles_in,
    slope_in,
    shift_in,
    image_out,
    shade_out,
    coarse,
    residual,
    levels,
    rank,
    angles,
    slope,
    shift,
    field16,
    field,
    low_halo,
    high_halo,
    edge,
    edge_left,
    edge_right,
    grad_x,
    grad_y,
    grad_z,
    tinted,
    pieces,
    arrived,
    shade_sum,
    image,
    load_sem,
    halo_send,
    halo_recv,
    piece_send,
    piece_recv,
    out_sem,
):
    dep, rows, cols = residual.shape
    me = lax.axis_index("depth")
    tile = lax.axis_index("tile")
    row_dev = rows // slabs
    per_piece = row_dev // SUB
    n_chunks = rows // SUB
    inner = min(n_chunks, cols // 4 // dep)
    n_blocks = n_chunks // inner
    block = inner * SUB
    step = 4.0 / (dep * slabs)

    barrier = pltpu.get_barrier_semaphore()
    for k in range(1, slabs):
        pl.semaphore_signal(
            barrier,
            inc=1,
            device_id=(lax.rem(me + k, slabs), tile),
            device_id_type=pl.DeviceIdType.MESH,
        )

    @pl.when(tile > 0)
    def _():
        pl.semaphore_signal(
            barrier, inc=1, device_id=(me, tile - 1), device_id_type=pl.DeviceIdType.MESH
        )

    @pl.when(tile < tiles - 1)
    def _():
        pl.semaphore_signal(
            barrier, inc=1, device_id=(me, tile + 1), device_id_type=pl.DeviceIdType.MESH
        )

    loads = [
        pltpu.make_async_copy(source, target, load_sem.at[i])
        for i, (source, target) in enumerate(
            [
                (residual_in, residual),
                (coarse_in, coarse),
                (levels_in, levels),
                (rank_in, rank),
                (angles_in, angles),
                (slope_in, slope),
                (shift_in, shift),
            ]
        )
    ]
    for load in loads:
        load.start()

    up_c = repeat_matrix((coarse.shape[2], cols), 1)
    up_r = repeat_matrix((rows, coarse.shape[1]), 0)
    level_c = repeat_matrix((levels.shape[2], cols), 1)
    level_r = repeat_matrix((rows, levels.shape[1]), 0)
    stencil = stencil_matrix(cols)
    lane = lax.broadcasted_iota(jnp.int32, (SUB, cols), 1)
    for z in range(dep):
        field[HALO + z, pl.ds(0, SUB), :] = jnp.zeros((SUB, cols), jnp.float32)
        field[HALO + z, pl.ds(SUB + rows, SUB), :] = jnp.zeros((SUB, cols), jnp.float32)
    for load in loads[1:]:
        load.wait()
    lifted = [
        matmul(up_r, matmul(coarse[z], up_c).astype(jnp.bfloat16)) for z in range(coarse.shape[0])
    ]
    scaled = [
        matmul(
            level_r,
            matmul((0.5 * levels[z].astype(jnp.float32)).astype(jnp.bfloat16), level_c).astype(
                jnp.bfloat16
            ),
        )
        for z in range(levels.shape[0])
    ]
    loads[0].wait()
    for z in range(dep):
        value = lifted[z * coarse.shape[0] // dep] + scaled[
            z * levels.shape[0] // dep
        ] * residual[z].astype(jnp.float32)
        rounded = value.astype(jnp.bfloat16)
        field16[z] = rounded
        field[HALO + z, pl.ds(SUB, rows), :] = rounded.astype(jnp.float32)

    def rows_of(q, i):
        start = q * block + i * SUB
        return start if isinstance(start, int) else pl.multiple_of(start, SUB)

    def pack(q):
        packed = jnp.zeros((SUB, cols), jnp.float32)
        for i in range(inner):
            for z in range(dep):
                j = i * dep + z
                value = field[HALO + z, pl.ds(SUB + rows_of(q, i), SUB), :]
                turned = pltpu.roll(value, (4 * j + HALO) % cols, 1)
                packed = jnp.where((lane >> 2) == j, turned, packed)
        edge[q] = packed

    each(n_blocks, pack)

    copies = [
        pltpu.make_async_remote_copy(
            source,
            target,
            halo_send.at[i],
            halo_recv.at[i],
            device_id=to,
            device_id_type=pl.DeviceIdType.MESH,
        )
        for i, (source, target, to) in enumerate(
            [
                (field16.at[pl.ds(dep - HALO, HALO)], low_halo, (me + 1, tile)),
                (field16.at[pl.ds(0, HALO)], high_halo, (me - 1, tile)),
                (edge, edge_left, (me, tile + 1)),
                (edge, edge_right, (me, tile - 1)),
            ]
        )
    ]
    can_send = [me < slabs - 1, me > 0, tile < tiles - 1, tile > 0]
    can_take = [me > 0, me < slabs - 1, tile > 0, tile < tiles - 1]
    landing = [low_halo, high_halo, edge_left, edge_right]

    pl.semaphore_wait(
        barrier, slabs - 1 + (tile > 0).astype(jnp.int32) + (tile < tiles - 1).astype(jnp.int32)
    )
    for copy, allowed in zip(copies, can_send):
        pl.when(allowed)(copy.start)
    for target, allowed in zip(landing, can_take):

        @pl.when(jnp.logical_not(allowed))
        def _():
            target[...] = jnp.zeros(target.shape, target.dtype)

    ascending = rank[0] < rank[slabs - 1]
    visible = jnp.where(rank[me] >= 0, 1.0, 0.0)
    azimuth = jnp.full((SUB, cols), angles[0], jnp.float32)
    elevation = jnp.full((SUB, cols), angles[1], jnp.float32)
    light_z = jnp.sin(elevation)
    light_y = jnp.cos(elevation) * jnp.sin(azimuth)
    light_x = jnp.cos(elevation) * jnp.cos(azimuth)

    for z in range(dep):
        grad_x[z] = matmul(field16[z], stencil)

    def halo_free(q):
        for i in range(inner):
            start = rows_of(q, i)
            here = pl.ds(start, SUB)
            value = [field[HALO + z, pl.ds(SUB + start, SUB), :] for z in range(dep)]
            for z in range(dep):

                def at(dy):
                    return field[HALO + z, pl.ds(SUB + start + dy, SUB), :]

                grad_y[z, here, :] = (at(-2) - at(2)) + 8.0 * (at(1) - at(-1))
                part = jnp.zeros((SUB, cols), jnp.float32)
                for dz, factor in ((-2, 1.0), (-1, -8.0), (1, 8.0), (2, -1.0)):
                    if 0 <= z + dz < dep:
                        part = part + factor * value[z + dz]
                grad_z[z, here, :] = part
            passed = [jnp.exp(-step * (2.0 + 2.0 * jnp.tanh(1.5 * (v - 1.5)))) for v in value]
            up, down = [None] * dep, [None] * dep
            up[0] = down[dep - 1] = jnp.ones((SUB, cols), jnp.float32)
            for z in range(1, dep):
                up[z] = up[z - 1] * passed[z - 1]
                down[dep - 1 - z] = down[dep - z] * passed[dep - z]
            for z in range(dep):
                weight = jnp.where(ascending, up[z], down[z]) * (1.0 - passed[z]) * visible
                for k in range(3):
                    colour = 0.5 + 0.5 * jnp.tanh(0.5 * (slope[k] * value[z] + shift[k]))
                    tinted[k, z, here, :] = weight * colour
            chunk = q * inner + i
            pieces[chunk // per_piece, 3, pl.ds(chunk % per_piece * SUB, SUB), :] = (
                1.0 - up[dep - 1] * passed[dep - 1]
            ) * visible

    each(n_blocks, halo_free)

    for copy, allowed in zip(copies, can_take):
        pl.when(allowed)(copy.wait_recv)

    def finish(q):
        left, right = edge_left[q], edge_right[q]
        place = lane & 3
        both = jnp.where(place < 2, left, right)
        outer = jnp.where(place < 2, -pltpu.roll(both, cols - 2, 1), pltpu.roll(both, 2, 1))
        near = jnp.where(
            place == 1,
            pltpu.roll(both, cols - 1, 1),
            jnp.where(place == 2, -pltpu.roll(both, 1, 1), 0.0),
        )
        fix = outer + 8.0 * near
        at_edge = (lane < HALO) | (lane >= cols - HALO)
        whole = q * block
        whole = whole if isinstance(whole, int) else pl.multiple_of(whole, block)
        low = [low_halo[z, pl.ds(whole, block), :].astype(jnp.float32) for z in range(HALO)]
        high = [high_halo[z, pl.ds(whole, block), :].astype(jnp.float32) for z in range(HALO)]
        for i in range(inner):
            here = pl.ds(rows_of(q, i), SUB)
            low_i = [v[i * SUB : (i + 1) * SUB] for v in low]
            high_i = [v[i * SUB : (i + 1) * SUB] for v in high]
            shades = []
            for z in range(dep):
                j = i * dep + z
                gx = grad_x[z, here, :] + jnp.where(
                    at_edge, pltpu.roll(fix, (cols - HALO - 4 * j) % cols, 1), 0.0
                )
                gy = grad_y[z, here, :]
                gz = grad_z[z, here, :]
                if z - 2 < 0:
                    gz = gz + low_i[z]
                if z - 1 < 0:
                    gz = gz - 8.0 * low_i[z + 1]
                if z + 1 >= dep:
                    gz = gz + 8.0 * high_i[z + 1 - dep]
                if z + 2 >= dep:
                    gz = gz - high_i[z + 2 - dep]
                along = light_z * gz + light_y * gy + light_x * gx
                square = gz * gz + gy * gy + gx * gx + 144.0
                shades.append(0.25 + 0.75 * jnp.abs(along) * lax.rsqrt(square))
            shade_sum[0, here, :] = sum(shades) * (1.0 / dep)
            chunk = q * inner + i
            for k in range(3):
                total = sum(tinted[k, z, here, :] * shades[z] for z in range(dep))
                pieces[chunk // per_piece, k, pl.ds(chunk % per_piece * SUB, SUB), :] = total

    each(n_blocks, finish)

    def piece_copy(other, slot):
        return pltpu.make_async_remote_copy(
            pieces.at[other],
            arrived.at[slot],
            piece_send.at[other],
            piece_recv.at[slot],
            device_id=(other, tile),
            device_id_type=pl.DeviceIdType.MESH,
        )

    others = [lax.rem(me + k, slabs) for k in range(1, slabs)]
    for other in others:
        piece_copy(other, me).start()
    shade_copy = pltpu.make_async_copy(shade_sum, shade_out, out_sem.at[0])
    shade_copy.start()
    arrived[me] = pieces[me]
    for other in others:
        piece_copy(other, other).wait_recv()
    total = [jnp.zeros((row_dev, cols), jnp.float32) for _ in range(3)]
    through = jnp.ones((row_dev, cols), jnp.float32)
    for s in range(slabs):
        layer = [
            jnp.where(ascending, arrived[s, k], arrived[slabs - 1 - s, k]) for k in range(4)
        ]
        total = [total[k] + through * layer[k] for k in range(3)]
        through = through * (1.0 - layer[3])
    for k in range(3):
        image[k] = total[k]
    image[3] = 1.0 - through
    image_copy = pltpu.make_async_copy(image, image_out, out_sem.at[1])
    image_copy.start()
    for copy, allowed in zip(copies, can_send):
        pl.when(allowed)(copy.wait_send)
    for other in others:
        piece_copy(other, me).wait_send()
    shade_copy.wait()
    image_copy.wait()


def shards(coarse, residual, levels, slab_rank, light_angles, color_slope, color_shift):
    dep, rows, cols = residual.shape
    slabs, tiles = lax.axis_size("depth"), lax.axis_size("tile")
    row_dev = rows // slabs
    n_chunks = rows // SUB
    n_blocks = n_chunks // min(n_chunks, cols // 4 // dep)
    f32, bf16 = jnp.float32, jnp.bfloat16
    hbm = pl.BlockSpec(memory_space=pl.ANY)
    dma = pltpu.SemaphoreType.DMA
    return pl.pallas_call(
        functools.partial(kernel, slabs, tiles),
        out_shape=(
            jax.ShapeDtypeStruct((4, row_dev, cols), f32),
            jax.ShapeDtypeStruct((1, rows, cols), f32),
        ),
        in_specs=[hbm] * 7,
        out_specs=(hbm, hbm),
        scratch_shapes=[
            pltpu.VMEM(coarse.shape, bf16),
            pltpu.VMEM(residual.shape, bf16),
            pltpu.VMEM(levels.shape, jnp.int32),
            pltpu.SMEM(slab_rank.shape, jnp.int32),
            pltpu.SMEM(light_angles.shape, f32),
            pltpu.SMEM(color_slope.shape, f32),
            pltpu.SMEM(color_shift.shape, f32),
            pltpu.VMEM((dep, rows, cols), bf16),
            pltpu.VMEM((dep + 2 * HALO, rows + 2 * SUB, cols), f32),
            pltpu.VMEM((HALO, rows, cols), bf16),
            pltpu.VMEM((HALO, rows, cols), bf16),
            pltpu.VMEM((n_blocks, SUB, cols), f32),
            pltpu.VMEM((n_blocks, SUB, cols), f32),
            pltpu.VMEM((n_blocks, SUB, cols), f32),
            pltpu.VMEM((dep, rows, cols), f32),
            pltpu.VMEM((dep, rows, cols), f32),
            pltpu.VMEM((dep, rows, cols), f32),
            pltpu.VMEM((3, dep, rows, cols), f32),
            pltpu.VMEM((slabs, 4, row_dev, cols), f32),
            pltpu.VMEM((slabs, 4, row_dev, cols), f32),
            pltpu.VMEM((1, rows, cols), f32),
            pltpu.VMEM((4, row_dev, cols), f32),
            dma((7,)),
            dma((4,)),
            dma((4,)),
            dma((slabs,)),
            dma((slabs,)),
            dma((2,)),
        ],
        compiler_params=pltpu.CompilerParams(
            collective_id=0, has_side_effects=True, vmem_limit_bytes=40 * 1024 * 1024
        ),
    )(coarse, residual, levels, slab_rank, light_angles, color_slope, color_shift)


def solution(mesh):
    placed = (
        P("depth", None, "tile"),
        P("depth", None, "tile"),
        P("depth", None, "tile"),
        P(),
        P(),
        P(),
        P(),
    )
    return jax.shard_map(
        shards,
        mesh=mesh,
        in_specs=placed,
        out_specs=(P(None, "depth", "tile"), P("depth", None, "tile")),
        check_vma=False,
    )
```

```python
import functools

import jax
import jax.numpy as jnp
from jax import lax
from jax.experimental import pallas as pl
from jax.experimental.pallas import tpu as pltpu
from jax.sharding import PartitionSpec as P

SUB = 8
HALO = 2


def each(count, body):
    if count == 1:
        body(0)
    else:
        lax.fori_loop(0, count, lambda i, _: (body(i), 0)[1], 0)


def repeat_matrix(shape, dim):
    factor = shape[dim] // shape[1 - dim]
    long = lax.broadcasted_iota(jnp.int32, shape, dim)
    short = lax.broadcasted_iota(jnp.int32, shape, 1 - dim) * factor
    return ((long >= short) & (long < short + factor)).astype(jnp.float32).astype(jnp.bfloat16)


def stencil_matrix(cols):
    apart = lax.broadcasted_iota(jnp.int32, (cols, cols), 0) - lax.broadcasted_iota(
        jnp.int32, (cols, cols), 1
    )
    value = jnp.where(apart == -2, 1.0, 0.0)
    value = jnp.where(apart == -1, -8.0, value)
    value = jnp.where(apart == 1, 8.0, value)
    value = jnp.where(apart == 2, -1.0, value)
    return value.astype(jnp.bfloat16)


def matmul(a, b):
    return jnp.dot(a, b, preferred_element_type=jnp.float32)


def kernel(
    slabs,
    tiles,
    coarse_in,
    residual_in,
    levels_in,
    rank_in,
    angles_in,
    slope_in,
    shift_in,
    image,
    shade_sum,
    coarse,
    residual,
    levels,
    rank,
    angles,
    slope,
    shift,
    field16,
    field,
    low_halo,
    high_halo,
    edge,
    edge_left,
    edge_right,
    grad_x,
    grad_y,
    grad_z,
    tinted,
    pieces,
    arrived,
    load_sem,
    halo_send,
    halo_recv,
    piece_send,
    piece_recv,
):
    dep, rows, cols = residual.shape
    me = lax.axis_index("depth")
    tile = lax.axis_index("tile")
    row_dev = rows // slabs
    per_piece = row_dev // SUB
    n_chunks = rows // SUB
    inner = min(n_chunks, cols // 4 // dep)
    n_blocks = n_chunks // inner
    block = inner * SUB
    step = 4.0 / (dep * slabs)

    barrier = pltpu.get_barrier_semaphore()
    for k in range(1, slabs):
        pl.semaphore_signal(
            barrier,
            inc=1,
            device_id=(lax.rem(me + k, slabs), tile),
            device_id_type=pl.DeviceIdType.MESH,
        )

    @pl.when(tile > 0)
    def _():
        pl.semaphore_signal(
            barrier, inc=1, device_id=(me, tile - 1), device_id_type=pl.DeviceIdType.MESH
        )

    @pl.when(tile < tiles - 1)
    def _():
        pl.semaphore_signal(
            barrier, inc=1, device_id=(me, tile + 1), device_id_type=pl.DeviceIdType.MESH
        )

    loads = [
        pltpu.make_async_copy(source, target, load_sem.at[i])
        for i, (source, target) in enumerate(
            [
                (residual_in, residual),
                (coarse_in, coarse),
                (levels_in, levels),
                (rank_in, rank),
                (angles_in, angles),
                (slope_in, slope),
                (shift_in, shift),
            ]
        )
    ]
    for load in loads:
        load.start()

    up_c = repeat_matrix((coarse.shape[2], cols), 1)
    up_r = repeat_matrix((rows, coarse.shape[1]), 0)
    level_c = repeat_matrix((levels.shape[2], cols), 1)
    level_r = repeat_matrix((rows, levels.shape[1]), 0)
    stencil = stencil_matrix(cols)
    lane = lax.broadcasted_iota(jnp.int32, (SUB, cols), 1)
    for z in range(dep):
        field[HALO + z, pl.ds(0, SUB), :] = jnp.zeros((SUB, cols), jnp.float32)
        field[HALO + z, pl.ds(SUB + rows, SUB), :] = jnp.zeros((SUB, cols), jnp.float32)
    for load in loads[1:]:
        load.wait()
    lifted = [
        matmul(up_r, matmul(coarse[z], up_c).astype(jnp.bfloat16)) for z in range(coarse.shape[0])
    ]
    scaled = [
        matmul(
            level_r,
            matmul((0.5 * levels[z].astype(jnp.float32)).astype(jnp.bfloat16), level_c).astype(
                jnp.bfloat16
            ),
        )
        for z in range(levels.shape[0])
    ]
    loads[0].wait()
    for z in range(dep):
        value = lifted[z * coarse.shape[0] // dep] + scaled[
            z * levels.shape[0] // dep
        ] * residual[z].astype(jnp.float32)
        rounded = value.astype(jnp.bfloat16)
        field16[z] = rounded
        field[HALO + z, pl.ds(SUB, rows), :] = rounded.astype(jnp.float32)

    def rows_of(q, i):
        start = q * block + i * SUB
        return start if isinstance(start, int) else pl.multiple_of(start, SUB)

    def pack(q):
        packed = jnp.zeros((SUB, cols), jnp.float32)
        for i in range(inner):
            for z in range(dep):
                j = i * dep + z
                value = field[HALO + z, pl.ds(SUB + rows_of(q, i), SUB), :]
                turned = pltpu.roll(value, (4 * j + HALO) % cols, 1)
                packed = jnp.where((lane >> 2) == j, turned, packed)
        edge[q] = packed

    each(n_blocks, pack)

    copies = [
        pltpu.make_async_remote_copy(
            source,
            target,
            halo_send.at[i],
            halo_recv.at[i],
            device_id=to,
            device_id_type=pl.DeviceIdType.MESH,
        )
        for i, (source, target, to) in enumerate(
            [
                (field16.at[pl.ds(dep - HALO, HALO)], low_halo, (me + 1, tile)),
                (field16.at[pl.ds(0, HALO)], high_halo, (me - 1, tile)),
                (edge, edge_left, (me, tile + 1)),
                (edge, edge_right, (me, tile - 1)),
            ]
        )
    ]
    can_send = [me < slabs - 1, me > 0, tile < tiles - 1, tile > 0]
    can_take = [me > 0, me < slabs - 1, tile > 0, tile < tiles - 1]
    landing = [low_halo, high_halo, edge_left, edge_right]

    pl.semaphore_wait(
        barrier, slabs - 1 + (tile > 0).astype(jnp.int32) + (tile < tiles - 1).astype(jnp.int32)
    )
    for copy, allowed in zip(copies, can_send):
        pl.when(allowed)(copy.start)
    for target, allowed in zip(landing, can_take):

        @pl.when(jnp.logical_not(allowed))
        def _():
            target[...] = jnp.zeros(target.shape, target.dtype)

    ascending = rank[0] < rank[slabs - 1]
    visible = jnp.where(rank[me] >= 0, 1.0, 0.0)
    azimuth = jnp.full((SUB, cols), angles[0], jnp.float32)
    elevation = jnp.full((SUB, cols), angles[1], jnp.float32)
    light_z = jnp.sin(elevation)
    light_y = jnp.cos(elevation) * jnp.sin(azimuth)
    light_x = jnp.cos(elevation) * jnp.cos(azimuth)

    for z in range(dep):
        grad_x[z] = matmul(field16[z], stencil)

    def halo_free(q):
        for i in range(inner):
            start = rows_of(q, i)
            here = pl.ds(start, SUB)
            value = [field[HALO + z, pl.ds(SUB + start, SUB), :] for z in range(dep)]
            for z in range(dep):

                def at(dy):
                    return field[HALO + z, pl.ds(SUB + start + dy, SUB), :]

                grad_y[z, here, :] = (at(-2) - at(2)) + 8.0 * (at(1) - at(-1))
                part = jnp.zeros((SUB, cols), jnp.float32)
                for dz, factor in ((-2, 1.0), (-1, -8.0), (1, 8.0), (2, -1.0)):
                    if 0 <= z + dz < dep:
                        part = part + factor * value[z + dz]
                grad_z[z, here, :] = part
            passed = [jnp.exp(-step * (2.0 + 2.0 * jnp.tanh(1.5 * (v - 1.5)))) for v in value]
            up, down = [None] * dep, [None] * dep
            up[0] = down[dep - 1] = jnp.ones((SUB, cols), jnp.float32)
            for z in range(1, dep):
                up[z] = up[z - 1] * passed[z - 1]
                down[dep - 1 - z] = down[dep - z] * passed[dep - z]
            for z in range(dep):
                weight = jnp.where(ascending, up[z], down[z]) * (1.0 - passed[z]) * visible
                for k in range(3):
                    colour = 0.5 + 0.5 * jnp.tanh(0.5 * (slope[k] * value[z] + shift[k]))
                    tinted[k, z, here, :] = weight * colour
            chunk = q * inner + i
            pieces[chunk // per_piece, 3, pl.ds(chunk % per_piece * SUB, SUB), :] = (
                1.0 - up[dep - 1] * passed[dep - 1]
            ) * visible

    each(n_blocks, halo_free)

    for copy, allowed in zip(copies, can_take):
        pl.when(allowed)(copy.wait_recv)

    def finish(q):
        left, right = edge_left[q], edge_right[q]
        place = lane & 3
        both = jnp.where(place < 2, left, right)
        outer = jnp.where(place < 2, -pltpu.roll(both, cols - 2, 1), pltpu.roll(both, 2, 1))
        near = jnp.where(
            place == 1,
            pltpu.roll(both, cols - 1, 1),
            jnp.where(place == 2, -pltpu.roll(both, 1, 1), 0.0),
        )
        fix = outer + 8.0 * near
        at_edge = (lane < HALO) | (lane >= cols - HALO)
        whole = q * block
        whole = whole if isinstance(whole, int) else pl.multiple_of(whole, block)
        low = [low_halo[z, pl.ds(whole, block), :].astype(jnp.float32) for z in range(HALO)]
        high = [high_halo[z, pl.ds(whole, block), :].astype(jnp.float32) for z in range(HALO)]
        for i in range(inner):
            here = pl.ds(rows_of(q, i), SUB)
            low_i = [v[i * SUB : (i + 1) * SUB] for v in low]
            high_i = [v[i * SUB : (i + 1) * SUB] for v in high]
            shades = []
            for z in range(dep):
                j = i * dep + z
                gx = grad_x[z, here, :] + jnp.where(
                    at_edge, pltpu.roll(fix, (cols - HALO - 4 * j) % cols, 1), 0.0
                )
                gy = grad_y[z, here, :]
                gz = grad_z[z, here, :]
                if z - 2 < 0:
                    gz = gz + low_i[z]
                if z - 1 < 0:
                    gz = gz - 8.0 * low_i[z + 1]
                if z + 1 >= dep:
                    gz = gz + 8.0 * high_i[z + 1 - dep]
                if z + 2 >= dep:
                    gz = gz - high_i[z + 2 - dep]
                along = light_z * gz + light_y * gy + light_x * gx
                square = gz * gz + gy * gy + gx * gx + 144.0
                shades.append(0.25 + 0.75 * jnp.abs(along) * lax.rsqrt(square))
            shade_sum[0, here, :] = sum(shades) * (1.0 / dep)
            chunk = q * inner + i
            for k in range(3):
                total = sum(tinted[k, z, here, :] * shades[z] for z in range(dep))
                pieces[chunk // per_piece, k, pl.ds(chunk % per_piece * SUB, SUB), :] = total

    each(n_blocks, finish)

    def piece_copy(other, slot):
        return pltpu.make_async_remote_copy(
            pieces.at[other],
            arrived.at[slot],
            piece_send.at[other],
            piece_recv.at[slot],
            device_id=(other, tile),
            device_id_type=pl.DeviceIdType.MESH,
        )

    others = [lax.rem(me + k, slabs) for k in range(1, slabs)]
    for other in others:
        piece_copy(other, me).start()
    arrived[me] = pieces[me]
    for other in others:
        piece_copy(other, other).wait_recv()
    total = [jnp.zeros((row_dev, cols), jnp.float32) for _ in range(3)]
    through = jnp.ones((row_dev, cols), jnp.float32)
    for s in range(slabs):
        layer = [
            jnp.where(ascending, arrived[s, k], arrived[slabs - 1 - s, k]) for k in range(4)
        ]
        total = [total[k] + through * layer[k] for k in range(3)]
        through = through * (1.0 - layer[3])
    for k in range(3):
        image[k] = total[k]
    image[3] = 1.0 - through
    for copy, allowed in zip(copies, can_send):
        pl.when(allowed)(copy.wait_send)
    for other in others:
        piece_copy(other, me).wait_send()


def shards(coarse, residual, levels, slab_rank, light_angles, color_slope, color_shift):
    dep, rows, cols = residual.shape
    slabs, tiles = lax.axis_size("depth"), lax.axis_size("tile")
    row_dev = rows // slabs
    n_chunks = rows // SUB
    n_blocks = n_chunks // min(n_chunks, cols // 4 // dep)
    f32, bf16 = jnp.float32, jnp.bfloat16
    hbm = pl.BlockSpec(memory_space=pltpu.HBM)
    vmem = pl.BlockSpec(memory_space=pltpu.VMEM)
    dma = pltpu.SemaphoreType.DMA
    return pl.pallas_call(
        functools.partial(kernel, slabs, tiles),
        out_shape=(
            pltpu.VMEM((4, row_dev, cols), f32),
            pltpu.VMEM((1, rows, cols), f32),
        ),
        in_specs=[hbm] * 7,
        out_specs=(vmem, vmem),
        scratch_shapes=[
            pltpu.VMEM(coarse.shape, bf16),
            pltpu.VMEM(residual.shape, bf16),
            pltpu.VMEM(levels.shape, jnp.int32),
            pltpu.SMEM(slab_rank.shape, jnp.int32),
            pltpu.SMEM(light_angles.shape, f32),
            pltpu.SMEM(color_slope.shape, f32),
            pltpu.SMEM(color_shift.shape, f32),
            pltpu.VMEM((dep, rows, cols), bf16),
            pltpu.VMEM((dep + 2 * HALO, rows + 2 * SUB, cols), f32),
            pltpu.VMEM((HALO, rows, cols), bf16),
            pltpu.VMEM((HALO, rows, cols), bf16),
            pltpu.VMEM((n_blocks, SUB, cols), f32),
            pltpu.VMEM((n_blocks, SUB, cols), f32),
            pltpu.VMEM((n_blocks, SUB, cols), f32),
            pltpu.VMEM((dep, rows, cols), f32),
            pltpu.VMEM((dep, rows, cols), f32),
            pltpu.VMEM((dep, rows, cols), f32),
            pltpu.VMEM((3, dep, rows, cols), f32),
            pltpu.VMEM((slabs, 4, row_dev, cols), f32),
            pltpu.VMEM((slabs, 4, row_dev, cols), f32),
            dma((7,)),
            dma((4,)),
            dma((4,)),
            dma((slabs,)),
            dma((slabs,)),
        ],
        compiler_params=pltpu.CompilerParams(
            collective_id=0, has_side_effects=True, vmem_limit_bytes=40 * 1024 * 1024
        ),
    )(
        *[
            pltpu.with_memory_space_constraint(x, pltpu.HBM)
            for x in (coarse, residual, levels, slab_rank, light_angles, color_slope, color_shift)
        ]
    )


def solution(mesh):
    placed = (
        P("depth", None, "tile"),
        P("depth", None, "tile"),
        P("depth", None, "tile"),
        P(),
        P(),
        P(),
        P(),
    )
    return jax.shard_map(
        shards,
        mesh=mesh,
        in_specs=placed,
        out_specs=(P(None, "depth", "tile"), P("depth", None, "tile")),
        check_vma=False,
    )
```

```python
import functools

import jax
import jax.numpy as jnp
from jax import lax
from jax.experimental import pallas as pl
from jax.experimental.pallas import tpu as pltpu
from jax.sharding import PartitionSpec as P

SUB = 8
HALO = 2


def each(count, body):
    if count == 1:
        body(0)
    else:
        lax.fori_loop(0, count, lambda i, _: (body(i), 0)[1], 0)


def repeat_matrix(shape, dim):
    factor = shape[dim] // shape[1 - dim]
    long = lax.broadcasted_iota(jnp.int32, shape, dim)
    short = lax.broadcasted_iota(jnp.int32, shape, 1 - dim) * factor
    return ((long >= short) & (long < short + factor)).astype(jnp.float32).astype(jnp.bfloat16)


def stencil_matrix(cols):
    apart = lax.broadcasted_iota(jnp.int32, (cols, cols), 0) - lax.broadcasted_iota(
        jnp.int32, (cols, cols), 1
    )
    value = jnp.where(apart == -2, 1.0, 0.0)
    value = jnp.where(apart == -1, -8.0, value)
    value = jnp.where(apart == 1, 8.0, value)
    value = jnp.where(apart == 2, -1.0, value)
    return value.astype(jnp.bfloat16)


def matmul(a, b):
    return jnp.dot(a, b, preferred_element_type=jnp.float32)


def kernel(
    slabs,
    tiles,
    coarse_in,
    residual_in,
    levels_in,
    rank_in,
    angles_in,
    slope_in,
    shift_in,
    image,
    shade_sum,
    coarse,
    residual,
    levels,
    rank,
    angles,
    slope,
    shift,
    field16,
    field,
    low_halo,
    high_halo,
    edge,
    edge_left,
    edge_right,
    grad_x,
    grad_y,
    grad_z,
    tinted,
    pieces,
    arrived,
    load_sem,
    halo_send,
    halo_recv,
    piece_send,
    piece_recv,
):
    dep, rows, cols = residual.shape
    me = lax.axis_index("depth")
    tile = lax.axis_index("tile")
    row_dev = rows // slabs
    per_piece = row_dev // SUB
    n_chunks = rows // SUB
    inner = min(n_chunks, cols // 4 // dep)
    n_blocks = n_chunks // inner
    block = inner * SUB
    step = 4.0 / (dep * slabs)

    loads = [
        pltpu.make_async_copy(source, target, load_sem.at[i])
        for i, (source, target) in enumerate(
            [
                (residual_in, residual),
                (coarse_in, coarse),
                (levels_in, levels),
                (rank_in, rank),
                (angles_in, angles),
                (slope_in, slope),
                (shift_in, shift),
            ]
        )
    ]
    for load in loads[:3]:
        load.start()

    barrier = pltpu.get_barrier_semaphore()
    for k in range(1, slabs):
        pl.semaphore_signal(
            barrier,
            inc=1,
            device_id=(lax.rem(me + k, slabs), tile),
            device_id_type=pl.DeviceIdType.MESH,
        )

    @pl.when(tile > 0)
    def _():
        pl.semaphore_signal(
            barrier, inc=1, device_id=(me, tile - 1), device_id_type=pl.DeviceIdType.MESH
        )

    @pl.when(tile < tiles - 1)
    def _():
        pl.semaphore_signal(
            barrier, inc=1, device_id=(me, tile + 1), device_id_type=pl.DeviceIdType.MESH
        )

    for load in loads[3:]:
        load.start()

    up_c = repeat_matrix((coarse.shape[2], cols), 1)
    up_r = repeat_matrix((rows, coarse.shape[1]), 0)
    level_c = repeat_matrix((levels.shape[2], cols), 1)
    level_r = repeat_matrix((rows, levels.shape[1]), 0)
    stencil = stencil_matrix(cols)
    lane = lax.broadcasted_iota(jnp.int32, (SUB, cols), 1)
    for z in range(dep):
        field[HALO + z, pl.ds(0, SUB), :] = jnp.zeros((SUB, cols), jnp.float32)
        field[HALO + z, pl.ds(SUB + rows, SUB), :] = jnp.zeros((SUB, cols), jnp.float32)
    for load in loads[1:3]:
        load.wait()
    lifted = [
        matmul(up_r, matmul(coarse[z], up_c).astype(jnp.bfloat16)) for z in range(coarse.shape[0])
    ]
    scaled = [
        matmul(
            level_r,
            matmul((0.5 * levels[z].astype(jnp.float32)).astype(jnp.bfloat16), level_c).astype(
                jnp.bfloat16
            ),
        )
        for z in range(levels.shape[0])
    ]
    loads[0].wait()
    for z in range(dep):
        value = lifted[z * coarse.shape[0] // dep] + scaled[
            z * levels.shape[0] // dep
        ] * residual[z].astype(jnp.float32)
        rounded = value.astype(jnp.bfloat16)
        field16[z] = rounded
        field[HALO + z, pl.ds(SUB, rows), :] = rounded.astype(jnp.float32)

    def rows_of(q, i):
        start = q * block + i * SUB
        return start if isinstance(start, int) else pl.multiple_of(start, SUB)

    def pack(q):
        packed = jnp.zeros((SUB, cols), jnp.float32)
        for i in range(inner):
            for z in range(dep):
                j = i * dep + z
                value = field[HALO + z, pl.ds(SUB + rows_of(q, i), SUB), :]
                turned = pltpu.roll(value, (4 * j + HALO) % cols, 1)
                packed = jnp.where((lane >> 2) == j, turned, packed)
        edge[q] = packed

    each(n_blocks, pack)

    copies = [
        pltpu.make_async_remote_copy(
            source,
            target,
            halo_send.at[i],
            halo_recv.at[i],
            device_id=to,
            device_id_type=pl.DeviceIdType.MESH,
        )
        for i, (source, target, to) in enumerate(
            [
                (field16.at[pl.ds(dep - HALO, HALO)], low_halo, (me + 1, tile)),
                (field16.at[pl.ds(0, HALO)], high_halo, (me - 1, tile)),
                (edge, edge_left, (me, tile + 1)),
                (edge, edge_right, (me, tile - 1)),
            ]
        )
    ]
    can_send = [me < slabs - 1, me > 0, tile < tiles - 1, tile > 0]
    can_take = [me > 0, me < slabs - 1, tile > 0, tile < tiles - 1]
    landing = [low_halo, high_halo, edge_left, edge_right]

    pl.semaphore_wait(
        barrier, slabs - 1 + (tile > 0).astype(jnp.int32) + (tile < tiles - 1).astype(jnp.int32)
    )
    for copy, allowed in zip(copies, can_send):
        pl.when(allowed)(copy.start)
    for target, allowed in zip(landing, can_take):

        @pl.when(jnp.logical_not(allowed))
        def _():
            target[...] = jnp.zeros(target.shape, target.dtype)

    for load in loads[3:]:
        load.wait()
    ascending = rank[0] < rank[slabs - 1]
    visible = jnp.where(rank[me] >= 0, 1.0, 0.0)
    azimuth = jnp.full((SUB, cols), angles[0], jnp.float32)
    elevation = jnp.full((SUB, cols), angles[1], jnp.float32)
    light_z = jnp.sin(elevation)
    light_y = jnp.cos(elevation) * jnp.sin(azimuth)
    light_x = jnp.cos(elevation) * jnp.cos(azimuth)

    for z in range(dep):
        grad_x[z] = matmul(field16[z], stencil)

    def halo_free(q):
        for i in range(inner):
            start = rows_of(q, i)
            here = pl.ds(start, SUB)
            value = [field[HALO + z, pl.ds(SUB + start, SUB), :] for z in range(dep)]
            for z in range(dep):

                def at(dy):
                    return field[HALO + z, pl.ds(SUB + start + dy, SUB), :]

                grad_y[z, here, :] = (at(-2) - at(2)) + 8.0 * (at(1) - at(-1))
                part = jnp.zeros((SUB, cols), jnp.float32)
                for dz, factor in ((-2, 1.0), (-1, -8.0), (1, 8.0), (2, -1.0)):
                    if 0 <= z + dz < dep:
                        part = part + factor * value[z + dz]
                grad_z[z, here, :] = part
            passed = [jnp.exp(-step * (2.0 + 2.0 * jnp.tanh(1.5 * (v - 1.5)))) for v in value]
            up, down = [None] * dep, [None] * dep
            up[0] = down[dep - 1] = jnp.ones((SUB, cols), jnp.float32)
            for z in range(1, dep):
                up[z] = up[z - 1] * passed[z - 1]
                down[dep - 1 - z] = down[dep - z] * passed[dep - z]
            for z in range(dep):
                weight = jnp.where(ascending, up[z], down[z]) * (1.0 - passed[z]) * visible
                for k in range(3):
                    colour = 0.5 + 0.5 * jnp.tanh(0.5 * (slope[k] * value[z] + shift[k]))
                    tinted[k, z, here, :] = weight * colour
            chunk = q * inner + i
            pieces[chunk // per_piece, 3, pl.ds(chunk % per_piece * SUB, SUB), :] = (
                1.0 - up[dep - 1] * passed[dep - 1]
            ) * visible

    each(n_blocks, halo_free)

    for copy, allowed in zip(copies, can_take):
        pl.when(allowed)(copy.wait_recv)

    def finish(q):
        left, right = edge_left[q], edge_right[q]
        place = lane & 3
        both = jnp.where(place < 2, left, right)
        outer = jnp.where(place < 2, -pltpu.roll(both, cols - 2, 1), pltpu.roll(both, 2, 1))
        near = jnp.where(
            place == 1,
            pltpu.roll(both, cols - 1, 1),
            jnp.where(place == 2, -pltpu.roll(both, 1, 1), 0.0),
        )
        fix = outer + 8.0 * near
        at_edge = (lane < HALO) | (lane >= cols - HALO)
        whole = q * block
        whole = whole if isinstance(whole, int) else pl.multiple_of(whole, block)
        low = [low_halo[z, pl.ds(whole, block), :].astype(jnp.float32) for z in range(HALO)]
        high = [high_halo[z, pl.ds(whole, block), :].astype(jnp.float32) for z in range(HALO)]
        for i in range(inner):
            here = pl.ds(rows_of(q, i), SUB)
            low_i = [v[i * SUB : (i + 1) * SUB] for v in low]
            high_i = [v[i * SUB : (i + 1) * SUB] for v in high]
            shades = []
            for z in range(dep):
                j = i * dep + z
                gx = grad_x[z, here, :] + jnp.where(
                    at_edge, pltpu.roll(fix, (cols - HALO - 4 * j) % cols, 1), 0.0
                )
                gy = grad_y[z, here, :]
                gz = grad_z[z, here, :]
                if z - 2 < 0:
                    gz = gz + low_i[z]
                if z - 1 < 0:
                    gz = gz - 8.0 * low_i[z + 1]
                if z + 1 >= dep:
                    gz = gz + 8.0 * high_i[z + 1 - dep]
                if z + 2 >= dep:
                    gz = gz - high_i[z + 2 - dep]
                along = light_z * gz + light_y * gy + light_x * gx
                square = gz * gz + gy * gy + gx * gx + 144.0
                shades.append(0.25 + 0.75 * jnp.abs(along) * lax.rsqrt(square))
            shade_sum[0, here, :] = sum(shades) * (1.0 / dep)
            chunk = q * inner + i
            for k in range(3):
                total = sum(tinted[k, z, here, :] * shades[z] for z in range(dep))
                pieces[chunk // per_piece, k, pl.ds(chunk % per_piece * SUB, SUB), :] = total

    each(n_blocks, finish)

    def piece_copy(other, slot):
        return pltpu.make_async_remote_copy(
            pieces.at[other],
            arrived.at[slot],
            piece_send.at[other],
            piece_recv.at[slot],
            device_id=(other, tile),
            device_id_type=pl.DeviceIdType.MESH,
        )

    others = [lax.rem(me + k, slabs) for k in range(1, slabs)]
    for other in others:
        piece_copy(other, me).start()
    arrived[me] = pieces[me]
    for other in others:
        piece_copy(other, other).wait_recv()
    total = [jnp.zeros((row_dev, cols), jnp.float32) for _ in range(3)]
    through = jnp.ones((row_dev, cols), jnp.float32)
    for s in range(slabs):
        layer = [
            jnp.where(ascending, arrived[s, k], arrived[slabs - 1 - s, k]) for k in range(4)
        ]
        total = [total[k] + through * layer[k] for k in range(3)]
        through = through * (1.0 - layer[3])
    for k in range(3):
        image[k] = total[k]
    image[3] = 1.0 - through
    for copy, allowed in zip(copies, can_send):
        pl.when(allowed)(copy.wait_send)
    for other in others:
        piece_copy(other, me).wait_send()


def store(image, shade, image_out, shade_out, sem):
    copies = [
        pltpu.make_async_copy(image, image_out, sem.at[0]),
        pltpu.make_async_copy(shade, shade_out, sem.at[1]),
    ]
    for copy in copies:
        copy.start()
    for copy in copies:
        copy.wait()


def shards(coarse, residual, levels, slab_rank, light_angles, color_slope, color_shift):
    dep, rows, cols = residual.shape
    slabs, tiles = lax.axis_size("depth"), lax.axis_size("tile")
    row_dev = rows // slabs
    n_chunks = rows // SUB
    n_blocks = n_chunks // min(n_chunks, cols // 4 // dep)
    f32, bf16 = jnp.float32, jnp.bfloat16
    hbm = pl.BlockSpec(memory_space=pltpu.HBM)
    vmem = pl.BlockSpec(memory_space=pltpu.VMEM)
    dma = pltpu.SemaphoreType.DMA
    image, shade = pl.pallas_call(
        functools.partial(kernel, slabs, tiles),
        out_shape=(
            pltpu.VMEM((4, row_dev, cols), f32),
            pltpu.VMEM((1, rows, cols), f32),
        ),
        in_specs=[hbm] * 7,
        out_specs=(vmem, vmem),
        scratch_shapes=[
            pltpu.VMEM(coarse.shape, bf16),
            pltpu.VMEM(residual.shape, bf16),
            pltpu.VMEM(levels.shape, jnp.int32),
            pltpu.SMEM(slab_rank.shape, jnp.int32),
            pltpu.SMEM(light_angles.shape, f32),
            pltpu.SMEM(color_slope.shape, f32),
            pltpu.SMEM(color_shift.shape, f32),
            pltpu.VMEM((dep, rows, cols), bf16),
            pltpu.VMEM((dep + 2 * HALO, rows + 2 * SUB, cols), f32),
            pltpu.VMEM((HALO, rows, cols), bf16),
            pltpu.VMEM((HALO, rows, cols), bf16),
            pltpu.VMEM((n_blocks, SUB, cols), f32),
            pltpu.VMEM((n_blocks, SUB, cols), f32),
            pltpu.VMEM((n_blocks, SUB, cols), f32),
            pltpu.VMEM((dep, rows, cols), f32),
            pltpu.VMEM((dep, rows, cols), f32),
            pltpu.VMEM((dep, rows, cols), f32),
            pltpu.VMEM((3, dep, rows, cols), f32),
            pltpu.VMEM((slabs, 4, row_dev, cols), f32),
            pltpu.VMEM((slabs, 4, row_dev, cols), f32),
            dma((7,)),
            dma((4,)),
            dma((4,)),
            dma((slabs,)),
            dma((slabs,)),
        ],
        compiler_params=pltpu.CompilerParams(
            collective_id=0, has_side_effects=True, vmem_limit_bytes=40 * 1024 * 1024
        ),
    )(
        *[
            pltpu.with_memory_space_constraint(x, pltpu.HBM)
            for x in (coarse, residual, levels, slab_rank, light_angles, color_slope, color_shift)
        ]
    )
    return pl.pallas_call(
        store,
        out_shape=(pltpu.HBM(image.shape, f32), pltpu.HBM(shade.shape, f32)),
        in_specs=[vmem] * 2,
        out_specs=(hbm, hbm),
        scratch_shapes=[dma((2,))],
    )(*[pltpu.with_memory_space_constraint(x, pltpu.VMEM) for x in (image, shade)])


def solution(mesh):
    placed = (
        P("depth", None, "tile"),
        P("depth", None, "tile"),
        P("depth", None, "tile"),
        P(),
        P(),
        P(),
        P(),
    )
    return jax.shard_map(
        shards,
        mesh=mesh,
        in_specs=placed,
        out_specs=(P(None, "depth", "tile"), P("depth", None, "tile")),
        check_vma=False,
    )
```

```python
import functools

import jax
import jax.numpy as jnp
from jax import lax
from jax.experimental import pallas as pl
from jax.experimental.pallas import tpu as pltpu
from jax.sharding import PartitionSpec as P

SUB = 8
HALO = 2


def each(count, body):
    if count == 1:
        body(0)
    else:
        lax.fori_loop(0, count, lambda i, _: (body(i), 0)[1], 0)


def repeat_matrix(shape, dim):
    factor = shape[dim] // shape[1 - dim]
    long = lax.broadcasted_iota(jnp.int32, shape, dim)
    short = lax.broadcasted_iota(jnp.int32, shape, 1 - dim) * factor
    return ((long >= short) & (long < short + factor)).astype(jnp.float32).astype(jnp.bfloat16)


def stencil_matrix(cols):
    apart = lax.broadcasted_iota(jnp.int32, (cols, cols), 0) - lax.broadcasted_iota(
        jnp.int32, (cols, cols), 1
    )
    value = jnp.where(apart == -2, 1.0, 0.0)
    value = jnp.where(apart == -1, -8.0, value)
    value = jnp.where(apart == 1, 8.0, value)
    value = jnp.where(apart == 2, -1.0, value)
    return value.astype(jnp.bfloat16)


def root(x):
    return x * lax.rsqrt(jnp.maximum(x, 1e-30))


def coded(value):
    level = root(root(value)) * 65535.0 + 0.5
    return jnp.minimum(level, 65535.0).astype(jnp.int32)


def pair_up(first, second):
    return (coded(first) << 16) | coded(second)


def decoded(word):
    halves = ((word >> 16) & 65535, word & 65535)
    roots = [half.astype(jnp.float32) * (1.0 / 65535.0) for half in halves]
    return [(r * r) * (r * r) for r in roots]


def matmul(a, b):
    return jnp.dot(a, b, preferred_element_type=jnp.float32)


def kernel(
    slabs,
    tiles,
    coarse_in,
    residual_in,
    levels_in,
    rank_in,
    angles_in,
    slope_in,
    shift_in,
    image,
    shade_sum,
    coarse,
    residual,
    levels,
    rank,
    angles,
    slope,
    shift,
    field16,
    field,
    low_halo,
    high_halo,
    edge,
    edge_left,
    edge_right,
    grad_x,
    grad_y,
    grad_z,
    tinted,
    veil,
    pieces,
    arrived,
    load_sem,
    halo_send,
    halo_recv,
    piece_send,
    piece_recv,
):
    dep, rows, cols = residual.shape
    me = lax.axis_index("depth")
    tile = lax.axis_index("tile")
    row_dev = rows // slabs
    per_piece = row_dev // SUB
    n_chunks = rows // SUB
    inner = min(n_chunks, cols // 4 // dep)
    n_blocks = n_chunks // inner
    block = inner * SUB
    step = 4.0 / (dep * slabs)

    loads = [
        pltpu.make_async_copy(source, target, load_sem.at[i])
        for i, (source, target) in enumerate(
            [
                (residual_in, residual),
                (coarse_in, coarse),
                (levels_in, levels),
                (rank_in, rank),
                (angles_in, angles),
                (slope_in, slope),
                (shift_in, shift),
            ]
        )
    ]
    for load in loads[:3]:
        load.start()

    barrier = pltpu.get_barrier_semaphore()
    for k in range(1, slabs):
        pl.semaphore_signal(
            barrier,
            inc=1,
            device_id=(lax.rem(me + k, slabs), tile),
            device_id_type=pl.DeviceIdType.MESH,
        )

    @pl.when(tile > 0)
    def _():
        pl.semaphore_signal(
            barrier, inc=1, device_id=(me, tile - 1), device_id_type=pl.DeviceIdType.MESH
        )

    @pl.when(tile < tiles - 1)
    def _():
        pl.semaphore_signal(
            barrier, inc=1, device_id=(me, tile + 1), device_id_type=pl.DeviceIdType.MESH
        )

    for load in loads[3:]:
        load.start()

    up_c = repeat_matrix((coarse.shape[2], cols), 1)
    up_r = repeat_matrix((rows, coarse.shape[1]), 0)
    level_c = repeat_matrix((levels.shape[2], cols), 1)
    level_r = repeat_matrix((rows, levels.shape[1]), 0)
    stencil = stencil_matrix(cols)
    lane = lax.broadcasted_iota(jnp.int32, (SUB, cols), 1)
    for z in range(dep):
        field[HALO + z, pl.ds(0, SUB), :] = jnp.zeros((SUB, cols), jnp.float32)
        field[HALO + z, pl.ds(SUB + rows, SUB), :] = jnp.zeros((SUB, cols), jnp.float32)
    for load in loads[1:3]:
        load.wait()
    lifted = [
        matmul(up_r, matmul(coarse[z], up_c).astype(jnp.bfloat16)) for z in range(coarse.shape[0])
    ]
    scaled = [
        matmul(
            level_r,
            matmul((0.5 * levels[z].astype(jnp.float32)).astype(jnp.bfloat16), level_c).astype(
                jnp.bfloat16
            ),
        )
        for z in range(levels.shape[0])
    ]
    loads[0].wait()
    for z in range(dep):
        value = lifted[z * coarse.shape[0] // dep] + scaled[
            z * levels.shape[0] // dep
        ] * residual[z].astype(jnp.float32)
        rounded = value.astype(jnp.bfloat16)
        field16[z] = rounded
        field[HALO + z, pl.ds(SUB, rows), :] = rounded.astype(jnp.float32)

    def rows_of(q, i):
        start = q * block + i * SUB
        return start if isinstance(start, int) else pl.multiple_of(start, SUB)

    def pack(q):
        packed = jnp.zeros((SUB, cols), jnp.float32)
        for i in range(inner):
            for z in range(dep):
                j = i * dep + z
                value = field[HALO + z, pl.ds(SUB + rows_of(q, i), SUB), :]
                turned = pltpu.roll(value, (4 * j + HALO) % cols, 1)
                packed = jnp.where((lane >> 2) == j, turned, packed)
        edge[q] = packed

    each(n_blocks, pack)

    copies = [
        pltpu.make_async_remote_copy(
            source,
            target,
            halo_send.at[i],
            halo_recv.at[i],
            device_id=to,
            device_id_type=pl.DeviceIdType.MESH,
        )
        for i, (source, target, to) in enumerate(
            [
                (field16.at[pl.ds(dep - HALO, HALO)], low_halo, (me + 1, tile)),
                (field16.at[pl.ds(0, HALO)], high_halo, (me - 1, tile)),
                (edge, edge_left, (me, tile + 1)),
                (edge, edge_right, (me, tile - 1)),
            ]
        )
    ]
    can_send = [me < slabs - 1, me > 0, tile < tiles - 1, tile > 0]
    can_take = [me > 0, me < slabs - 1, tile > 0, tile < tiles - 1]
    landing = [low_halo, high_halo, edge_left, edge_right]

    pl.semaphore_wait(
        barrier, slabs - 1 + (tile > 0).astype(jnp.int32) + (tile < tiles - 1).astype(jnp.int32)
    )
    for copy, allowed in zip(copies, can_send):
        pl.when(allowed)(copy.start)
    for target, allowed in zip(landing, can_take):

        @pl.when(jnp.logical_not(allowed))
        def _():
            target[...] = jnp.zeros(target.shape, target.dtype)

    for load in loads[3:]:
        load.wait()
    ascending = rank[0] < rank[slabs - 1]
    visible = jnp.where(rank[me] >= 0, 1.0, 0.0)
    azimuth = jnp.full((SUB, cols), angles[0], jnp.float32)
    elevation = jnp.full((SUB, cols), angles[1], jnp.float32)
    light_z = jnp.sin(elevation)
    light_y = jnp.cos(elevation) * jnp.sin(azimuth)
    light_x = jnp.cos(elevation) * jnp.cos(azimuth)

    for z in range(dep):
        grad_x[z] = matmul(field16[z], stencil)

    def halo_free(q):
        for i in range(inner):
            start = rows_of(q, i)
            here = pl.ds(start, SUB)
            value = [field[HALO + z, pl.ds(SUB + start, SUB), :] for z in range(dep)]
            for z in range(dep):

                def at(dy):
                    return field[HALO + z, pl.ds(SUB + start + dy, SUB), :]

                grad_y[z, here, :] = (at(-2) - at(2)) + 8.0 * (at(1) - at(-1))
                part = jnp.zeros((SUB, cols), jnp.float32)
                for dz, factor in ((-2, 1.0), (-1, -8.0), (1, 8.0), (2, -1.0)):
                    if 0 <= z + dz < dep:
                        part = part + factor * value[z + dz]
                grad_z[z, here, :] = part
            passed = [jnp.exp(-step * (2.0 + 2.0 * jnp.tanh(1.5 * (v - 1.5)))) for v in value]
            up, down = [None] * dep, [None] * dep
            up[0] = down[dep - 1] = jnp.ones((SUB, cols), jnp.float32)
            for z in range(1, dep):
                up[z] = up[z - 1] * passed[z - 1]
                down[dep - 1 - z] = down[dep - z] * passed[dep - z]
            for z in range(dep):
                weight = jnp.where(ascending, up[z], down[z]) * (1.0 - passed[z]) * visible
                for k in range(3):
                    colour = 0.5 + 0.5 * jnp.tanh(0.5 * (slope[k] * value[z] + shift[k]))
                    tinted[k, z, here, :] = weight * colour
            veil[here, :] = (1.0 - up[dep - 1] * passed[dep - 1]) * visible

    each(n_blocks, halo_free)

    for copy, allowed in zip(copies, can_take):
        pl.when(allowed)(copy.wait_recv)

    def finish(q):
        left, right = edge_left[q], edge_right[q]
        place = lane & 3
        both = jnp.where(place < 2, left, right)
        outer = jnp.where(place < 2, -pltpu.roll(both, cols - 2, 1), pltpu.roll(both, 2, 1))
        near = jnp.where(
            place == 1,
            pltpu.roll(both, cols - 1, 1),
            jnp.where(place == 2, -pltpu.roll(both, 1, 1), 0.0),
        )
        fix = outer + 8.0 * near
        at_edge = (lane < HALO) | (lane >= cols - HALO)
        whole = q * block
        whole = whole if isinstance(whole, int) else pl.multiple_of(whole, block)
        low = [low_halo[z, pl.ds(whole, block), :].astype(jnp.float32) for z in range(HALO)]
        high = [high_halo[z, pl.ds(whole, block), :].astype(jnp.float32) for z in range(HALO)]
        for i in range(inner):
            here = pl.ds(rows_of(q, i), SUB)
            low_i = [v[i * SUB : (i + 1) * SUB] for v in low]
            high_i = [v[i * SUB : (i + 1) * SUB] for v in high]
            shades = []
            for z in range(dep):
                j = i * dep + z
                gx = grad_x[z, here, :] + jnp.where(
                    at_edge, pltpu.roll(fix, (cols - HALO - 4 * j) % cols, 1), 0.0
                )
                gy = grad_y[z, here, :]
                gz = grad_z[z, here, :]
                if z - 2 < 0:
                    gz = gz + low_i[z]
                if z - 1 < 0:
                    gz = gz - 8.0 * low_i[z + 1]
                if z + 1 >= dep:
                    gz = gz + 8.0 * high_i[z + 1 - dep]
                if z + 2 >= dep:
                    gz = gz - high_i[z + 2 - dep]
                along = light_z * gz + light_y * gy + light_x * gx
                square = gz * gz + gy * gy + gx * gx + 144.0
                shades.append(0.25 + 0.75 * jnp.abs(along) * lax.rsqrt(square))
            shade_sum[0, here, :] = sum(shades) * (1.0 / dep)
            chunk = q * inner + i
            totals = [sum(tinted[k, z, here, :] * shades[z] for z in range(dep)) for k in range(3)]
            totals.append(veil[here, :])
            for k in range(2):
                pieces[chunk // per_piece, k, pl.ds(chunk % per_piece * SUB, SUB), :] = pair_up(
                    totals[2 * k], totals[2 * k + 1]
                )

    each(n_blocks, finish)

    def piece_copy(other, slot):
        return pltpu.make_async_remote_copy(
            pieces.at[other],
            arrived.at[slot],
            piece_send.at[other],
            piece_recv.at[slot],
            device_id=(other, tile),
            device_id_type=pl.DeviceIdType.MESH,
        )

    others = [lax.rem(me + k, slabs) for k in range(1, slabs)]
    for other in others:
        piece_copy(other, me).start()
    arrived[me] = pieces[me]
    for other in others:
        piece_copy(other, other).wait_recv()
    total = [jnp.zeros((row_dev, cols), jnp.float32) for _ in range(3)]
    through = jnp.ones((row_dev, cols), jnp.float32)
    for s in range(slabs):
        words = [
            jnp.where(ascending, arrived[s, k], arrived[slabs - 1 - s, k]) for k in range(2)
        ]
        layer = decoded(words[0]) + decoded(words[1])
        total = [total[k] + through * layer[k] for k in range(3)]
        through = through * (1.0 - layer[3])
    for k in range(3):
        image[k] = total[k]
    image[3] = 1.0 - through
    for copy, allowed in zip(copies, can_send):
        pl.when(allowed)(copy.wait_send)
    for other in others:
        piece_copy(other, me).wait_send()


def store(image, shade, image_out, shade_out, sem):
    copies = [
        pltpu.make_async_copy(image, image_out, sem.at[0]),
        pltpu.make_async_copy(shade, shade_out, sem.at[1]),
    ]
    for copy in copies:
        copy.start()
    for copy in copies:
        copy.wait()


def shards(coarse, residual, levels, slab_rank, light_angles, color_slope, color_shift):
    dep, rows, cols = residual.shape
    slabs, tiles = lax.axis_size("depth"), lax.axis_size("tile")
    row_dev = rows // slabs
    n_chunks = rows // SUB
    n_blocks = n_chunks // min(n_chunks, cols // 4 // dep)
    f32, bf16 = jnp.float32, jnp.bfloat16
    hbm = pl.BlockSpec(memory_space=pltpu.HBM)
    vmem = pl.BlockSpec(memory_space=pltpu.VMEM)
    dma = pltpu.SemaphoreType.DMA
    image, shade = pl.pallas_call(
        functools.partial(kernel, slabs, tiles),
        out_shape=(
            pltpu.VMEM((4, row_dev, cols), f32),
            pltpu.VMEM((1, rows, cols), f32),
        ),
        in_specs=[hbm] * 7,
        out_specs=(vmem, vmem),
        scratch_shapes=[
            pltpu.VMEM(coarse.shape, bf16),
            pltpu.VMEM(residual.shape, bf16),
            pltpu.VMEM(levels.shape, jnp.int32),
            pltpu.SMEM(slab_rank.shape, jnp.int32),
            pltpu.SMEM(light_angles.shape, f32),
            pltpu.SMEM(color_slope.shape, f32),
            pltpu.SMEM(color_shift.shape, f32),
            pltpu.VMEM((dep, rows, cols), bf16),
            pltpu.VMEM((dep + 2 * HALO, rows + 2 * SUB, cols), f32),
            pltpu.VMEM((HALO, rows, cols), bf16),
            pltpu.VMEM((HALO, rows, cols), bf16),
            pltpu.VMEM((n_blocks, SUB, cols), f32),
            pltpu.VMEM((n_blocks, SUB, cols), f32),
            pltpu.VMEM((n_blocks, SUB, cols), f32),
            pltpu.VMEM((dep, rows, cols), f32),
            pltpu.VMEM((dep, rows, cols), f32),
            pltpu.VMEM((dep, rows, cols), f32),
            pltpu.VMEM((3, dep, rows, cols), f32),
            pltpu.VMEM((rows, cols), f32),
            pltpu.VMEM((slabs, 2, row_dev, cols), jnp.int32),
            pltpu.VMEM((slabs, 2, row_dev, cols), jnp.int32),
            dma((7,)),
            dma((4,)),
            dma((4,)),
            dma((slabs,)),
            dma((slabs,)),
        ],
        compiler_params=pltpu.CompilerParams(
            collective_id=0, has_side_effects=True, vmem_limit_bytes=40 * 1024 * 1024
        ),
    )(
        *[
            pltpu.with_memory_space_constraint(x, pltpu.HBM)
            for x in (coarse, residual, levels, slab_rank, light_angles, color_slope, color_shift)
        ]
    )
    return pl.pallas_call(
        store,
        out_shape=(pltpu.HBM(image.shape, f32), pltpu.HBM(shade.shape, f32)),
        in_specs=[vmem] * 2,
        out_specs=(hbm, hbm),
        scratch_shapes=[dma((2,))],
    )(*[pltpu.with_memory_space_constraint(x, pltpu.VMEM) for x in (image, shade)])


def solution(mesh):
    placed = (
        P("depth", None, "tile"),
        P("depth", None, "tile"),
        P("depth", None, "tile"),
        P(),
        P(),
        P(),
        P(),
    )
    return jax.shard_map(
        shards,
        mesh=mesh,
        in_specs=placed,
        out_specs=(P(None, "depth", "tile"), P("depth", None, "tile")),
        check_vma=False,
    )
```

```python
import functools

import jax
import jax.numpy as jnp
from jax import lax
from jax.experimental import pallas as pl
from jax.experimental.pallas import tpu as pltpu
from jax.sharding import PartitionSpec as P

SUB = 8
HALO = 2


def each(count, body):
    if count == 1:
        body(0)
    else:
        lax.fori_loop(0, count, lambda i, _: (body(i), 0)[1], 0)


def repeat_matrix(shape, dim):
    factor = shape[dim] // shape[1 - dim]
    long = lax.broadcasted_iota(jnp.int32, shape, dim)
    short = lax.broadcasted_iota(jnp.int32, shape, 1 - dim) * factor
    return ((long >= short) & (long < short + factor)).astype(jnp.float32).astype(jnp.bfloat16)


def stencil_matrix(cols):
    apart = lax.broadcasted_iota(jnp.int32, (cols, cols), 0) - lax.broadcasted_iota(
        jnp.int32, (cols, cols), 1
    )
    value = jnp.where(apart == -2, 1.0, 0.0)
    value = jnp.where(apart == -1, -8.0, value)
    value = jnp.where(apart == 1, 8.0, value)
    value = jnp.where(apart == 2, -1.0, value)
    return value.astype(jnp.bfloat16)


def root(x):
    return x * lax.rsqrt(jnp.maximum(x, 1e-30))


def coded(value):
    level = root(root(value)) * 65535.0 + 0.5
    return jnp.minimum(level, 65535.0).astype(jnp.int32)


def pair_up(first, second):
    return (coded(first) << 16) | coded(second)


def decoded(word):
    halves = ((word >> 16) & 65535, word & 65535)
    roots = [half.astype(jnp.float32) * (1.0 / 65535.0) for half in halves]
    return [(r * r) * (r * r) for r in roots]


def matmul(a, b):
    return jnp.dot(a, b, preferred_element_type=jnp.float32)


def kernel(
    slabs,
    tiles,
    coarse_in,
    residual_in,
    levels_in,
    rank_in,
    angles_in,
    slope_in,
    shift_in,
    image,
    shade_sum,
    coarse,
    residual,
    levels,
    rank,
    angles,
    slope,
    shift,
    field16,
    field,
    low_halo,
    high_halo,
    edge,
    edge_left,
    edge_right,
    grad_x,
    grad_y,
    grad_z,
    tinted,
    veil,
    pieces,
    arrived,
    load_sem,
    halo_send,
    halo_recv,
    piece_send,
    piece_recv,
):
    dep, rows, cols = residual.shape
    me = lax.axis_index("depth")
    tile = lax.axis_index("tile")
    row_dev = rows // slabs
    per_piece = row_dev // SUB
    n_chunks = rows // SUB
    inner = min(n_chunks, cols // 4 // dep)
    n_blocks = n_chunks // inner
    block = inner * SUB
    step = 4.0 / (dep * slabs)

    loads = [
        pltpu.make_async_copy(source, target, load_sem.at[i])
        for i, (source, target) in enumerate(
            [
                (residual_in, residual),
                (coarse_in, coarse),
                (levels_in, levels),
                (rank_in, rank),
                (angles_in, angles),
                (slope_in, slope),
                (shift_in, shift),
            ]
        )
    ]
    for load in loads[:3]:
        load.start()

    barrier = pltpu.get_barrier_semaphore()
    order = sorted(range(1, slabs), key=lambda k: min(k, slabs - k))
    for k in order:
        pl.semaphore_signal(
            barrier,
            inc=1,
            device_id=(lax.rem(me + k, slabs), tile),
            device_id_type=pl.DeviceIdType.MESH,
        )

    @pl.when(tile > 0)
    def _():
        pl.semaphore_signal(
            barrier, inc=1, device_id=(me, tile - 1), device_id_type=pl.DeviceIdType.MESH
        )

    @pl.when(tile < tiles - 1)
    def _():
        pl.semaphore_signal(
            barrier, inc=1, device_id=(me, tile + 1), device_id_type=pl.DeviceIdType.MESH
        )

    for load in loads[3:]:
        load.start()

    up_c = repeat_matrix((coarse.shape[2], cols), 1)
    up_r = repeat_matrix((rows, coarse.shape[1]), 0)
    level_c = repeat_matrix((levels.shape[2], cols), 1)
    level_r = repeat_matrix((rows, levels.shape[1]), 0)
    stencil = stencil_matrix(cols)
    lane = lax.broadcasted_iota(jnp.int32, (SUB, cols), 1)
    for z in range(dep):
        field[HALO + z, pl.ds(0, SUB), :] = jnp.zeros((SUB, cols), jnp.float32)
        field[HALO + z, pl.ds(SUB + rows, SUB), :] = jnp.zeros((SUB, cols), jnp.float32)
    for load in loads[1:3]:
        load.wait()
    lifted = [
        matmul(up_r, matmul(coarse[z], up_c).astype(jnp.bfloat16)) for z in range(coarse.shape[0])
    ]
    scaled = [
        matmul(
            level_r,
            matmul((0.5 * levels[z].astype(jnp.float32)).astype(jnp.bfloat16), level_c).astype(
                jnp.bfloat16
            ),
        )
        for z in range(levels.shape[0])
    ]
    loads[0].wait()
    for z in range(dep):
        value = lifted[z * coarse.shape[0] // dep] + scaled[
            z * levels.shape[0] // dep
        ] * residual[z].astype(jnp.float32)
        rounded = value.astype(jnp.bfloat16)
        field16[z] = rounded
        field[HALO + z, pl.ds(SUB, rows), :] = rounded.astype(jnp.float32)

    def rows_of(q, i):
        start = q * block + i * SUB
        return start if isinstance(start, int) else pl.multiple_of(start, SUB)

    def pack(q):
        packed = jnp.zeros((SUB, cols), jnp.float32)
        for i in range(inner):
            for z in range(dep):
                j = i * dep + z
                value = field[HALO + z, pl.ds(SUB + rows_of(q, i), SUB), :]
                turned = pltpu.roll(value, (4 * j + HALO) % cols, 1)
                packed = jnp.where((lane >> 2) == j, turned, packed)
        edge[q] = packed

    each(n_blocks, pack)

    copies = [
        pltpu.make_async_remote_copy(
            source,
            target,
            halo_send.at[i],
            halo_recv.at[i],
            device_id=to,
            device_id_type=pl.DeviceIdType.MESH,
        )
        for i, (source, target, to) in enumerate(
            [
                (field16.at[pl.ds(dep - HALO, HALO)], low_halo, (me + 1, tile)),
                (field16.at[pl.ds(0, HALO)], high_halo, (me - 1, tile)),
                (edge, edge_left, (me, tile + 1)),
                (edge, edge_right, (me, tile - 1)),
            ]
        )
    ]
    can_send = [me < slabs - 1, me > 0, tile < tiles - 1, tile > 0]
    can_take = [me > 0, me < slabs - 1, tile > 0, tile < tiles - 1]
    landing = [low_halo, high_halo, edge_left, edge_right]

    pl.semaphore_wait(
        barrier, slabs - 1 + (tile > 0).astype(jnp.int32) + (tile < tiles - 1).astype(jnp.int32)
    )
    for copy, allowed in zip(copies, can_send):
        pl.when(allowed)(copy.start)
    for target, allowed in zip(landing, can_take):

        @pl.when(jnp.logical_not(allowed))
        def _():
            target[...] = jnp.zeros(target.shape, target.dtype)

    for load in loads[3:]:
        load.wait()
    ascending = rank[0] < rank[slabs - 1]
    visible = jnp.where(rank[me] >= 0, 1.0, 0.0)
    azimuth = jnp.full((SUB, cols), angles[0], jnp.float32)
    elevation = jnp.full((SUB, cols), angles[1], jnp.float32)
    light_z = jnp.sin(elevation)
    light_y = jnp.cos(elevation) * jnp.sin(azimuth)
    light_x = jnp.cos(elevation) * jnp.cos(azimuth)

    for z in range(dep):
        grad_x[z] = matmul(field16[z], stencil)

    def halo_free(q):
        for i in range(inner):
            start = rows_of(q, i)
            here = pl.ds(start, SUB)
            value = [field[HALO + z, pl.ds(SUB + start, SUB), :] for z in range(dep)]
            for z in range(dep):

                def at(dy):
                    return field[HALO + z, pl.ds(SUB + start + dy, SUB), :]

                grad_y[z, here, :] = (at(-2) - at(2)) + 8.0 * (at(1) - at(-1))
                part = jnp.zeros((SUB, cols), jnp.float32)
                for dz, factor in ((-2, 1.0), (-1, -8.0), (1, 8.0), (2, -1.0)):
                    if 0 <= z + dz < dep:
                        part = part + factor * value[z + dz]
                grad_z[z, here, :] = part
            passed = [jnp.exp(-step * (2.0 + 2.0 * jnp.tanh(1.5 * (v - 1.5)))) for v in value]
            up, down = [None] * dep, [None] * dep
            up[0] = down[dep - 1] = jnp.ones((SUB, cols), jnp.float32)
            for z in range(1, dep):
                up[z] = up[z - 1] * passed[z - 1]
                down[dep - 1 - z] = down[dep - z] * passed[dep - z]
            for z in range(dep):
                weight = jnp.where(ascending, up[z], down[z]) * (1.0 - passed[z]) * visible
                for k in range(3):
                    colour = 0.5 + 0.5 * jnp.tanh(0.5 * (slope[k] * value[z] + shift[k]))
                    tinted[k, z, here, :] = weight * colour
            veil[here, :] = (1.0 - up[dep - 1] * passed[dep - 1]) * visible

    each(n_blocks, halo_free)

    for copy, allowed in zip(copies, can_take):
        pl.when(allowed)(copy.wait_recv)

    def piece_copy(other, slot):
        return pltpu.make_async_remote_copy(
            pieces.at[other],
            arrived.at[slot],
            piece_send.at[other],
            piece_recv.at[slot],
            device_id=(other, tile),
            device_id_type=pl.DeviceIdType.MESH,
        )

    def finish(q):
        left, right = edge_left[q], edge_right[q]
        place = lane & 3
        both = jnp.where(place < 2, left, right)
        outer = jnp.where(place < 2, -pltpu.roll(both, cols - 2, 1), pltpu.roll(both, 2, 1))
        near = jnp.where(
            place == 1,
            pltpu.roll(both, cols - 1, 1),
            jnp.where(place == 2, -pltpu.roll(both, 1, 1), 0.0),
        )
        fix = outer + 8.0 * near
        at_edge = (lane < HALO) | (lane >= cols - HALO)
        whole = q * block
        whole = whole if isinstance(whole, int) else pl.multiple_of(whole, block)
        low = [low_halo[z, pl.ds(whole, block), :].astype(jnp.float32) for z in range(HALO)]
        high = [high_halo[z, pl.ds(whole, block), :].astype(jnp.float32) for z in range(HALO)]
        for i in range(inner):
            here = pl.ds(rows_of(q, i), SUB)
            low_i = [v[i * SUB : (i + 1) * SUB] for v in low]
            high_i = [v[i * SUB : (i + 1) * SUB] for v in high]
            shades = []
            for z in range(dep):
                j = i * dep + z
                gx = grad_x[z, here, :] + jnp.where(
                    at_edge, pltpu.roll(fix, (cols - HALO - 4 * j) % cols, 1), 0.0
                )
                gy = grad_y[z, here, :]
                gz = grad_z[z, here, :]
                if z - 2 < 0:
                    gz = gz + low_i[z]
                if z - 1 < 0:
                    gz = gz - 8.0 * low_i[z + 1]
                if z + 1 >= dep:
                    gz = gz + 8.0 * high_i[z + 1 - dep]
                if z + 2 >= dep:
                    gz = gz - high_i[z + 2 - dep]
                along = light_z * gz + light_y * gy + light_x * gx
                square = gz * gz + gy * gy + gx * gx + 144.0
                shades.append(0.25 + 0.75 * jnp.abs(along) * lax.rsqrt(square))
            shade_sum[0, here, :] = sum(shades) * (1.0 / dep)
            chunk = q * inner + i
            totals = [sum(tinted[k, z, here, :] * shades[z] for z in range(dep)) for k in range(3)]
            totals.append(veil[here, :])
            for k in range(2):
                pieces[chunk // per_piece, k, pl.ds(chunk % per_piece * SUB, SUB), :] = pair_up(
                    totals[2 * k], totals[2 * k + 1]
                )
            if (i + 1) % per_piece == 0:
                piece = chunk // per_piece
                pl.when(piece != me)(piece_copy(piece, me).start)

    each(n_blocks, finish)

    others = [lax.rem(me + k, slabs) for k in range(1, slabs)]
    arrived[me] = pieces[me]
    for other in others:
        piece_copy(other, other).wait_recv()
    total = [jnp.zeros((row_dev, cols), jnp.float32) for _ in range(3)]
    through = jnp.ones((row_dev, cols), jnp.float32)
    for s in range(slabs):
        words = [
            jnp.where(ascending, arrived[s, k], arrived[slabs - 1 - s, k]) for k in range(2)
        ]
        layer = decoded(words[0]) + decoded(words[1])
        total = [total[k] + through * layer[k] for k in range(3)]
        through = through * (1.0 - layer[3])
    for k in range(3):
        image[k] = total[k]
    image[3] = 1.0 - through
    for copy, allowed in zip(copies, can_send):
        pl.when(allowed)(copy.wait_send)
    for other in others:
        piece_copy(other, me).wait_send()


def store(image, shade, image_out, shade_out, sem):
    copies = [
        pltpu.make_async_copy(image, image_out, sem.at[0]),
        pltpu.make_async_copy(shade, shade_out, sem.at[1]),
    ]
    for copy in copies:
        copy.start()
    for copy in copies:
        copy.wait()


def shards(coarse, residual, levels, slab_rank, light_angles, color_slope, color_shift):
    dep, rows, cols = residual.shape
    slabs, tiles = lax.axis_size("depth"), lax.axis_size("tile")
    row_dev = rows // slabs
    n_chunks = rows // SUB
    n_blocks = n_chunks // min(n_chunks, cols // 4 // dep)
    f32, bf16 = jnp.float32, jnp.bfloat16
    hbm = pl.BlockSpec(memory_space=pltpu.HBM)
    vmem = pl.BlockSpec(memory_space=pltpu.VMEM)
    dma = pltpu.SemaphoreType.DMA
    image, shade = pl.pallas_call(
        functools.partial(kernel, slabs, tiles),
        out_shape=(
            pltpu.VMEM((4, row_dev, cols), f32),
            pltpu.VMEM((1, rows, cols), f32),
        ),
        in_specs=[hbm] * 7,
        out_specs=(vmem, vmem),
        scratch_shapes=[
            pltpu.VMEM(coarse.shape, bf16),
            pltpu.VMEM(residual.shape, bf16),
            pltpu.VMEM(levels.shape, jnp.int32),
            pltpu.SMEM(slab_rank.shape, jnp.int32),
            pltpu.SMEM(light_angles.shape, f32),
            pltpu.SMEM(color_slope.shape, f32),
            pltpu.SMEM(color_shift.shape, f32),
            pltpu.VMEM((dep, rows, cols), bf16),
            pltpu.VMEM((dep + 2 * HALO, rows + 2 * SUB, cols), f32),
            pltpu.VMEM((HALO, rows, cols), bf16),
            pltpu.VMEM((HALO, rows, cols), bf16),
            pltpu.VMEM((n_blocks, SUB, cols), f32),
            pltpu.VMEM((n_blocks, SUB, cols), f32),
            pltpu.VMEM((n_blocks, SUB, cols), f32),
            pltpu.VMEM((dep, rows, cols), f32),
            pltpu.VMEM((dep, rows, cols), f32),
            pltpu.VMEM((dep, rows, cols), f32),
            pltpu.VMEM((3, dep, rows, cols), f32),
            pltpu.VMEM((rows, cols), f32),
            pltpu.VMEM((slabs, 2, row_dev, cols), jnp.int32),
            pltpu.VMEM((slabs, 2, row_dev, cols), jnp.int32),
            dma((7,)),
            dma((4,)),
            dma((4,)),
            dma((slabs,)),
            dma((slabs,)),
        ],
        compiler_params=pltpu.CompilerParams(
            collective_id=0, has_side_effects=True, vmem_limit_bytes=40 * 1024 * 1024
        ),
    )(
        *[
            pltpu.with_memory_space_constraint(x, pltpu.HBM)
            for x in (coarse, residual, levels, slab_rank, light_angles, color_slope, color_shift)
        ]
    )
    return pl.pallas_call(
        store,
        out_shape=(pltpu.HBM(image.shape, f32), pltpu.HBM(shade.shape, f32)),
        in_specs=[vmem] * 2,
        out_specs=(hbm, hbm),
        scratch_shapes=[dma((2,))],
    )(*[pltpu.with_memory_space_constraint(x, pltpu.VMEM) for x in (image, shade)])


def solution(mesh):
    placed = (
        P("depth", None, "tile"),
        P("depth", None, "tile"),
        P("depth", None, "tile"),
        P(),
        P(),
        P(),
        P(),
    )
    return jax.shard_map(
        shards,
        mesh=mesh,
        in_specs=placed,
        out_specs=(P(None, "depth", "tile"), P("depth", None, "tile")),
        check_vma=False,
    )
```

```python
import functools

import jax
import jax.numpy as jnp
from jax import lax
from jax.experimental import pallas as pl
from jax.experimental.pallas import tpu as pltpu
from jax.sharding import PartitionSpec as P

SUB = 8
HALO = 2


def each(count, body):
    if count == 1:
        body(0)
    else:
        lax.fori_loop(0, count, lambda i, _: (body(i), 0)[1], 0)


def repeat_matrix(shape, dim):
    factor = shape[dim] // shape[1 - dim]
    long = lax.broadcasted_iota(jnp.int32, shape, dim)
    short = lax.broadcasted_iota(jnp.int32, shape, 1 - dim) * factor
    return ((long >= short) & (long < short + factor)).astype(jnp.float32).astype(jnp.bfloat16)


def stencil_matrix(cols):
    apart = lax.broadcasted_iota(jnp.int32, (cols, cols), 0) - lax.broadcasted_iota(
        jnp.int32, (cols, cols), 1
    )
    value = jnp.where(apart == -2, 1.0, 0.0)
    value = jnp.where(apart == -1, -8.0, value)
    value = jnp.where(apart == 1, 8.0, value)
    value = jnp.where(apart == 2, -1.0, value)
    return value.astype(jnp.bfloat16)


def matmul(a, b):
    return jnp.dot(a, b, preferred_element_type=jnp.float32)


def edge_terms(left, right, lane):
    cols = left.shape[1]
    place = lane & 3
    both = jnp.where(place < 2, left, right)
    outer = jnp.where(place < 2, -pltpu.roll(both, cols - 2, 1), pltpu.roll(both, 2, 1))
    near = jnp.where(
        place == 1,
        pltpu.roll(both, cols - 1, 1),
        jnp.where(place == 2, -pltpu.roll(both, 1, 1), 0.0),
    )
    return outer + 8.0 * near


def kernel(
    slabs,
    tiles,
    coarse_in,
    residual_in,
    levels_in,
    rank_in,
    angles_in,
    slope_in,
    shift_in,
    image,
    shade_sum,
    coarse,
    residual,
    levels,
    rank,
    angles,
    slope,
    shift,
    field16,
    field,
    low_halo,
    high_halo,
    edge,
    edge_left,
    edge_right,
    rows_out,
    rows_left,
    rows_right,
    parts,
    parts_in,
    mine,
    mine_x,
    grad_x,
    grad_y,
    grad_z,
    load_sem,
    halo_send,
    halo_recv,
    part_send,
    part_recv,
    left_send,
    left_recv,
    right_send,
    right_recv,
):
    dep, rows, cols = residual.shape
    me = lax.axis_index("depth")
    tile = lax.axis_index("tile")
    n_chunks = rows // SUB
    inner = min(n_chunks, cols // 4 // dep)
    n_blocks = n_chunks // inner
    block = inner * SUB
    main = dep * SUB
    step = 4.0 / (dep * slabs)
    mesh_id = pl.DeviceIdType.MESH
    has_left, has_right = tile > 0, tile < tiles - 1

    loads = [
        pltpu.make_async_copy(source, target, load_sem.at[i])
        for i, (source, target) in enumerate(
            [
                (residual_in, residual),
                (coarse_in, coarse),
                (levels_in, levels),
                (rank_in, rank),
                (angles_in, angles),
                (slope_in, slope),
                (shift_in, shift),
            ]
        )
    ]
    for load in loads[:3]:
        load.start()

    barrier = pltpu.get_barrier_semaphore()
    for k in range(1, slabs):
        pl.semaphore_signal(
            barrier, inc=1, device_id=(lax.rem(me + k, slabs), tile), device_id_type=mesh_id
        )
    for allowed, to in ((has_left, tile - 1), (has_right, tile + 1)):

        @pl.when(allowed)
        def _():
            for k in range(slabs):
                p = lax.rem(me + k, slabs)
                pl.semaphore_signal(barrier, inc=1, device_id=(p, to), device_id_type=mesh_id)

    for load in loads[3:]:
        load.start()

    up_c = repeat_matrix((coarse.shape[2], cols), 1)
    up_r = repeat_matrix((rows, coarse.shape[1]), 0)
    level_c = repeat_matrix((levels.shape[2], cols), 1)
    level_r = repeat_matrix((rows, levels.shape[1]), 0)
    stencil = stencil_matrix(cols)
    lane = lax.broadcasted_iota(jnp.int32, (SUB, cols), 1)
    row = lax.broadcasted_iota(jnp.int32, (SUB, cols), 0)
    zero = jnp.zeros((SUB, cols), jnp.float32)
    for z in range(dep):
        field[z, pl.ds(0, SUB), :] = zero
        field[z, pl.ds(SUB + rows, SUB), :] = zero
    for g in (0, 1, HALO + slabs * dep, HALO + slabs * dep + 1):
        mine[g, pl.ds(SUB, SUB), :] = zero
    for load in loads[1:3]:
        load.wait()
    lifted = [
        matmul(up_r, matmul(coarse[z], up_c).astype(jnp.bfloat16)) for z in range(coarse.shape[0])
    ]
    scaled = [
        matmul(
            level_r,
            matmul((0.5 * levels[z].astype(jnp.float32)).astype(jnp.bfloat16), level_c).astype(
                jnp.bfloat16
            ),
        )
        for z in range(levels.shape[0])
    ]
    loads[0].wait()
    for z in range(dep):
        value = lifted[z * coarse.shape[0] // dep] + scaled[
            z * levels.shape[0] // dep
        ] * residual[z].astype(jnp.float32)
        rounded = value.astype(jnp.bfloat16)
        field16[z] = rounded
        field[z, pl.ds(SUB, rows), :] = rounded.astype(jnp.float32)

    def rows_of(q, i):
        start = q * block + i * SUB
        return start if isinstance(start, int) else pl.multiple_of(start, SUB)

    def pack(q):
        packed = zero
        for i in range(inner):
            start = rows_of(q, i)
            piece = q * inner + i

            def rows_at(z, offset):
                return field[z, pl.ds(SUB + start + offset, SUB), :]

            strips = []
            for z in range(0, dep, 2):
                for other in range(2):
                    j = i * dep + z + other
                    turned = pltpu.roll(rows_at(z + other, 0), (4 * j + HALO) % cols, 1)
                    packed = jnp.where((lane >> 2) == j, turned, packed)
                pair = jnp.concatenate([rows_at(z, 0), rows_at(z + 1, 0)], axis=0)
                parts[piece, z // 2] = pair.astype(jnp.bfloat16)
                strip = jnp.where(row >= 6, rows_at(z, -8), rows_at(z, 8))
                strip = jnp.where((row == 2) | (row == 3), rows_at(z + 1, -4), strip)
                strip = jnp.where((row == 4) | (row == 5), rows_at(z + 1, 4), strip)
                strips.append(strip)
            for k in range(dep // 4):
                pair = jnp.concatenate(strips[2 * k : 2 * k + 2], axis=0)
                parts[piece, dep // 2 + k] = pair.astype(jnp.bfloat16)
        edge[q] = packed
        for i in range(inner):
            rows_out[q * inner + i] = pltpu.roll(packed, -4 * dep * i % cols, 1)

    each(n_blocks, pack)

    copies = [
        pltpu.make_async_remote_copy(
            source, target, halo_send.at[i], halo_recv.at[i], device_id=to, device_id_type=mesh_id
        )
        for i, (source, target, to) in enumerate(
            [
                (field16.at[pl.ds(dep - HALO, HALO)], low_halo, (me + 1, tile)),
                (field16.at[pl.ds(0, HALO)], high_halo, (me - 1, tile)),
                (edge, edge_left, (me, tile + 1)),
                (edge, edge_right, (me, tile - 1)),
            ]
        )
    ]
    can_send = [me < slabs - 1, me > 0, has_right, has_left]
    can_take = [me > 0, me < slabs - 1, has_left, has_right]
    landing = [low_halo, high_halo, edge_left, edge_right]

    def part_copy(other, slot):
        return pltpu.make_async_remote_copy(
            parts.at[other],
            parts_in.at[slot],
            part_send.at[other],
            part_recv.at[slot],
            device_id=(other, tile),
            device_id_type=mesh_id,
        )

    def row_copy(other, slot, to_right, to):
        target, send, recv = (
            (rows_left, left_send, left_recv) if to_right else (rows_right, right_send, right_recv)
        )
        return pltpu.make_async_remote_copy(
            rows_out.at[other],
            target.at[slot],
            send.at[other],
            recv.at[slot],
            device_id=(other, to),
            device_id_type=mesh_id,
        )

    others = [lax.rem(me + k, slabs) for k in range(1, slabs)]
    pl.semaphore_wait(
        barrier,
        slabs - 1 + slabs * (has_left.astype(jnp.int32) + has_right.astype(jnp.int32)),
    )
    for other in others:
        part_copy(other, me).start()
    for to_right, allowed, to in ((True, has_right, tile + 1), (False, has_left, tile - 1)):

        @pl.when(allowed)
        def _():
            for p in [me] + others:
                row_copy(p, me, to_right, to).start()

    for copy, allowed in zip(copies, can_send):
        pl.when(allowed)(copy.start)
    for target, allowed in zip(
        landing + [rows_left, rows_right], can_take + [has_left, has_right]
    ):

        @pl.when(jnp.logical_not(allowed))
        def _():
            target[...] = jnp.zeros(target.shape, target.dtype)

    parts_in[me] = parts[me]
    for load in loads[3:]:
        load.wait()
    ascending = rank[0] < rank[slabs - 1]
    azimuth = jnp.full((SUB, cols), angles[0], jnp.float32)
    elevation = jnp.full((SUB, cols), angles[1], jnp.float32)
    light_z = jnp.sin(elevation)
    light_y = jnp.cos(elevation) * jnp.sin(azimuth)
    light_x = jnp.cos(elevation) * jnp.cos(azimuth)
    at_edge = (lane < HALO) | (lane >= cols - HALO)

    def shading(gz, gy, gx):
        along = light_z * gz + light_y * gy + light_x * gx
        square = gz * gz + gy * gy + gx * gx + 144.0
        return 0.25 + 0.75 * jnp.abs(along) * lax.rsqrt(square)

    def corrected(gx, fix, j):
        return gx + jnp.where(at_edge, pltpu.roll(fix, (cols - HALO - 4 * j) % cols, 1), 0.0)

    for z in range(dep):
        grad_x[z] = matmul(field16[z], stencil)

    def halo_free(q):
        for i in range(inner):
            start = rows_of(q, i)
            here = pl.ds(start, SUB)
            value = [field[z, pl.ds(SUB + start, SUB), :] for z in range(dep)]
            for z in range(dep):

                def at(dy):
                    return field[z, pl.ds(SUB + start + dy, SUB), :]

                grad_y[z, here, :] = (at(-2) - at(2)) + 8.0 * (at(1) - at(-1))
                part = zero
                for dz, factor in ((-2, 1.0), (-1, -8.0), (1, 8.0), (2, -1.0)):
                    if 0 <= z + dz < dep:
                        part = part + factor * value[z + dz]
                grad_z[z, here, :] = part

    each(n_blocks, halo_free)

    for other in others:
        part_copy(other, other).wait_recv()
    for to_right, allowed, to in ((True, has_left, tile - 1), (False, has_right, tile + 1)):

        @pl.when(allowed)
        def _():
            for p in [me] + others:
                row_copy(p, p, to_right, to).wait_recv()

    group = min(slabs, inner)
    n_groups = slabs // group

    def unpack(q):
        for i in range(group):
            s = q * group + i
            values = parts_in[s].astype(jnp.float32).reshape(main * 3 // 2, cols)
            for z in range(dep):
                g = HALO + s * dep + z
                first = main + z // 2 * SUB
                strip = values[first : first + SUB]
                if z % 2:
                    strip = pltpu.roll(strip, 4, 0)
                mine[g, pl.ds(0, SUB), :] = strip
                mine[g, pl.ds(SUB, SUB), :] = values[z * SUB : (z + 1) * SUB]
                mine[g, pl.ds(2 * SUB, SUB), :] = strip
        together = parts_in[pl.ds(q * group, group), pl.ds(0, dep // 2)]
        mine_x[pl.ds(q * group, group)] = matmul(
            together.reshape(group * main, cols), stencil
        ).reshape(group, main, cols)

    each(n_groups, unpack)

    def composite(q, carry):
        total, through = list(carry[:3]), carry[3]
        sides = []
        for arrived in (rows_left, rows_right):
            gathered = zero
            for i in range(group):
                turned = pltpu.roll(arrived[q * group + i], 4 * dep * i % cols, 1)
                gathered = jnp.where(lane // (4 * dep) == i, turned, gathered)
            sides.append(gathered)
        fix = edge_terms(*sides, lane)
        for i in range(group):
            s = q * group + i
            visible = rank[s] >= 0
            for z in range(dep):
                g = HALO + s * dep + z

                def at(dz, dy):
                    return mine[g + dz, pl.ds(SUB + dy, SUB), :]

                value = at(0, 0)
                gz = (at(-2, 0) - at(2, 0)) + 8.0 * (at(1, 0) - at(-1, 0))
                gy = (at(0, -2) - at(0, 2)) + 8.0 * (at(0, 1) - at(0, -1))
                gx = corrected(mine_x[s, pl.ds(z * SUB, SUB), :], fix, i * dep + z)
                passed = jnp.exp(-step * (2.0 + 2.0 * jnp.tanh(1.5 * (value - 1.5))))
                passed = jnp.where(visible, passed, 1.0)
                weight = (1.0 - passed) * shading(gz, gy, gx)
                factor_old = jnp.where(ascending, 1.0, passed)
                factor_new = jnp.where(ascending, through, 1.0) * weight
                for k in range(3):
                    colour = 0.5 + 0.5 * jnp.tanh(0.5 * (slope[k] * value + shift[k]))
                    total[k] = total[k] * factor_old + factor_new * colour
                through = through * passed
        return (*total, through)

    start = (zero, zero, zero, zero + 1.0)
    done = composite(0, start) if n_groups == 1 else lax.fori_loop(0, n_groups, composite, start)
    for k in range(3):
        image[k] = done[k]
    image[3] = 1.0 - done[3]

    for copy, allowed in zip(copies, can_take):
        pl.when(allowed)(copy.wait_recv)

    def finish(q):
        fix = edge_terms(edge_left[q], edge_right[q], lane)
        whole = q * block
        whole = whole if isinstance(whole, int) else pl.multiple_of(whole, block)
        low = [low_halo[z, pl.ds(whole, block), :].astype(jnp.float32) for z in range(HALO)]
        high = [high_halo[z, pl.ds(whole, block), :].astype(jnp.float32) for z in range(HALO)]
        for i in range(inner):
            here = pl.ds(rows_of(q, i), SUB)
            low_i = [v[i * SUB : (i + 1) * SUB] for v in low]
            high_i = [v[i * SUB : (i + 1) * SUB] for v in high]
            shades = []
            for z in range(dep):
                gx = corrected(grad_x[z, here, :], fix, i * dep + z)
                gz = grad_z[z, here, :]
                if z - 2 < 0:
                    gz = gz + low_i[z]
                if z - 1 < 0:
                    gz = gz - 8.0 * low_i[z + 1]
                if z + 1 >= dep:
                    gz = gz + 8.0 * high_i[z + 1 - dep]
                if z + 2 >= dep:
                    gz = gz - high_i[z + 2 - dep]
                shades.append(shading(gz, grad_y[z, here, :], gx))
            shade_sum[0, here, :] = sum(shades) * (1.0 / dep)

    each(n_blocks, finish)

    for copy, allowed in zip(copies, can_send):
        pl.when(allowed)(copy.wait_send)
    for other in others:
        part_copy(other, me).wait_send()
    for to_right, allowed, to in ((True, has_right, tile + 1), (False, has_left, tile - 1)):

        @pl.when(allowed)
        def _():
            for p in [me] + others:
                row_copy(p, me, to_right, to).wait_send()


def store(image, shade, image_out, shade_out, sem):
    copies = [
        pltpu.make_async_copy(image, image_out, sem.at[0]),
        pltpu.make_async_copy(shade, shade_out, sem.at[1]),
    ]
    for copy in copies:
        copy.start()
    for copy in copies:
        copy.wait()


def shards(coarse, residual, levels, slab_rank, light_angles, color_slope, color_shift):
    dep, rows, cols = residual.shape
    slabs, tiles = lax.axis_size("depth"), lax.axis_size("tile")
    row_dev = rows // slabs
    n_chunks = rows // SUB
    n_blocks = n_chunks // min(n_chunks, cols // 4 // dep)
    f32, bf16 = jnp.float32, jnp.bfloat16
    hbm = pl.BlockSpec(memory_space=pltpu.HBM)
    vmem = pl.BlockSpec(memory_space=pltpu.VMEM)
    dma = pltpu.SemaphoreType.DMA
    image, shade = pl.pallas_call(
        functools.partial(kernel, slabs, tiles),
        out_shape=(
            pltpu.VMEM((4, row_dev, cols), f32),
            pltpu.VMEM((1, rows, cols), f32),
        ),
        in_specs=[hbm] * 7,
        out_specs=(vmem, vmem),
        scratch_shapes=[
            pltpu.VMEM(coarse.shape, bf16),
            pltpu.VMEM(residual.shape, bf16),
            pltpu.VMEM(levels.shape, jnp.int32),
            pltpu.SMEM(slab_rank.shape, jnp.int32),
            pltpu.SMEM(light_angles.shape, f32),
            pltpu.SMEM(color_slope.shape, f32),
            pltpu.SMEM(color_shift.shape, f32),
            pltpu.VMEM((dep, rows, cols), bf16),
            pltpu.VMEM((dep, rows + 2 * SUB, cols), f32),
            pltpu.VMEM((HALO, rows, cols), bf16),
            pltpu.VMEM((HALO, rows, cols), bf16),
            pltpu.VMEM((n_blocks, SUB, cols), f32),
            pltpu.VMEM((n_blocks, SUB, cols), f32),
            pltpu.VMEM((n_blocks, SUB, cols), f32),
            pltpu.VMEM((slabs, SUB, cols), f32),
            pltpu.VMEM((slabs, SUB, cols), f32),
            pltpu.VMEM((slabs, SUB, cols), f32),
            pltpu.VMEM((slabs, dep * 3 // 4, 2 * SUB, cols), bf16),
            pltpu.VMEM((slabs, dep * 3 // 4, 2 * SUB, cols), bf16),
            pltpu.VMEM((slabs * dep + 2 * HALO, 4 * SUB, cols), f32),
            pltpu.VMEM((slabs, dep * SUB, cols), f32),
            pltpu.VMEM((dep, rows, cols), f32),
            pltpu.VMEM((dep, rows, cols), f32),
            pltpu.VMEM((dep, rows, cols), f32),
            dma((7,)),
            dma((4,)),
            dma((4,)),
            dma((slabs,)),
            dma((slabs,)),
            dma((slabs,)),
            dma((slabs,)),
            dma((slabs,)),
            dma((slabs,)),
        ],
        compiler_params=pltpu.CompilerParams(
            collective_id=0, has_side_effects=True, vmem_limit_bytes=40 * 1024 * 1024
        ),
    )(
        *[
            pltpu.with_memory_space_constraint(x, pltpu.HBM)
            for x in (coarse, residual, levels, slab_rank, light_angles, color_slope, color_shift)
        ]
    )
    return pl.pallas_call(
        store,
        out_shape=(pltpu.HBM(image.shape, f32), pltpu.HBM(shade.shape, f32)),
        in_specs=[vmem] * 2,
        out_specs=(hbm, hbm),
        scratch_shapes=[dma((2,))],
    )(*[pltpu.with_memory_space_constraint(x, pltpu.VMEM) for x in (image, shade)])


def solution(mesh):
    placed = (
        P("depth", None, "tile"),
        P("depth", None, "tile"),
        P("depth", None, "tile"),
        P(),
        P(),
        P(),
        P(),
    )
    return jax.shard_map(
        shards,
        mesh=mesh,
        in_specs=placed,
        out_specs=(P(None, "depth", "tile"), P("depth", None, "tile")),
        check_vma=False,
    )
```

```python
import functools

import jax
import jax.numpy as jnp
from jax import lax
from jax.experimental import pallas as pl
from jax.experimental.pallas import tpu as pltpu
from jax.sharding import PartitionSpec as P

SUB = 8
HALO = 2


def each(count, body):
    if count == 1:
        body(0)
    else:
        lax.fori_loop(0, count, lambda i, _: (body(i), 0)[1], 0)


def repeat_matrix(shape, dim):
    factor = shape[dim] // shape[1 - dim]
    long = lax.broadcasted_iota(jnp.int32, shape, dim)
    short = lax.broadcasted_iota(jnp.int32, shape, 1 - dim) * factor
    return ((long >= short) & (long < short + factor)).astype(jnp.float32).astype(jnp.bfloat16)


def stencil_matrix(cols):
    apart = lax.broadcasted_iota(jnp.int32, (cols, cols), 0) - lax.broadcasted_iota(
        jnp.int32, (cols, cols), 1
    )
    value = jnp.where(apart == -2, 1.0, 0.0)
    value = jnp.where(apart == -1, -8.0, value)
    value = jnp.where(apart == 1, 8.0, value)
    value = jnp.where(apart == 2, -1.0, value)
    return value.astype(jnp.bfloat16)


def matmul(a, b):
    return jnp.dot(a, b, preferred_element_type=jnp.float32)


def edge_terms(left, right, lane):
    cols = left.shape[1]
    place = lane & 3
    both = jnp.where(place < 2, left, right)
    outer = jnp.where(place < 2, -pltpu.roll(both, cols - 2, 1), pltpu.roll(both, 2, 1))
    near = jnp.where(
        place == 1,
        pltpu.roll(both, cols - 1, 1),
        jnp.where(place == 2, -pltpu.roll(both, 1, 1), 0.0),
    )
    return outer + 8.0 * near


def kernel(
    slabs,
    tiles,
    coarse_in,
    residual_in,
    levels_in,
    rank_in,
    angles_in,
    slope_in,
    shift_in,
    image,
    shade_sum,
    coarse,
    residual,
    levels,
    rank,
    angles,
    slope,
    shift,
    field16,
    field,
    low_halo,
    high_halo,
    edge,
    edge_left,
    edge_right,
    rows_out,
    rows_left,
    rows_right,
    parts,
    parts_in,
    mine,
    mine_x,
    grad_x,
    grad_y,
    grad_z,
    load_sem,
    halo_send,
    halo_recv,
    part_send,
    part_recv,
    left_send,
    left_recv,
    right_send,
    right_recv,
):
    dep, rows, cols = residual.shape
    me = lax.axis_index("depth")
    tile = lax.axis_index("tile")
    n_chunks = rows // SUB
    inner = min(n_chunks, cols // 4 // dep)
    n_blocks = n_chunks // inner
    block = inner * SUB
    main = dep * SUB
    step = 4.0 / (dep * slabs)
    mesh_id = pl.DeviceIdType.MESH
    has_left, has_right = tile > 0, tile < tiles - 1

    loads = [
        pltpu.make_async_copy(source, target, load_sem.at[i])
        for i, (source, target) in enumerate(
            [
                (residual_in, residual),
                (coarse_in, coarse),
                (levels_in, levels),
                (rank_in, rank),
                (angles_in, angles),
                (slope_in, slope),
                (shift_in, shift),
            ]
        )
    ]
    for load in loads[:3]:
        load.start()

    barrier = pltpu.get_barrier_semaphore()
    for k in range(1, slabs):
        pl.semaphore_signal(
            barrier, inc=1, device_id=(lax.rem(me + k, slabs), tile), device_id_type=mesh_id
        )
    for allowed, to in ((has_left, tile - 1), (has_right, tile + 1)):

        @pl.when(allowed)
        def _():
            for k in range(slabs):
                p = lax.rem(me + k, slabs)
                pl.semaphore_signal(barrier, inc=1, device_id=(p, to), device_id_type=mesh_id)

    for load in loads[3:]:
        load.start()

    up_c = repeat_matrix((coarse.shape[2], cols), 1)
    up_r = repeat_matrix((rows, coarse.shape[1]), 0)
    level_c = repeat_matrix((levels.shape[2], cols), 1)
    level_r = repeat_matrix((rows, levels.shape[1]), 0)
    stencil = stencil_matrix(cols)
    lane = lax.broadcasted_iota(jnp.int32, (SUB, cols), 1)
    row = lax.broadcasted_iota(jnp.int32, (SUB, cols), 0)
    zero = jnp.zeros((SUB, cols), jnp.float32)
    for z in range(dep):
        field[z, pl.ds(0, SUB), :] = zero
        field[z, pl.ds(SUB + rows, SUB), :] = zero
    for g in (0, 1, HALO + slabs * dep, HALO + slabs * dep + 1):
        mine[g, pl.ds(SUB, SUB), :] = zero
    for load in loads[1:3]:
        load.wait()
    lifted = [
        matmul(up_r, matmul(coarse[z], up_c).astype(jnp.bfloat16)) for z in range(coarse.shape[0])
    ]
    scaled = [
        matmul(
            level_r,
            matmul((0.5 * levels[z].astype(jnp.float32)).astype(jnp.bfloat16), level_c).astype(
                jnp.bfloat16
            ),
        )
        for z in range(levels.shape[0])
    ]
    loads[0].wait()
    for z in range(dep):
        value = lifted[z * coarse.shape[0] // dep] + scaled[
            z * levels.shape[0] // dep
        ] * residual[z].astype(jnp.float32)
        rounded = value.astype(jnp.bfloat16)
        field16[z] = rounded
        field[z, pl.ds(SUB, rows), :] = rounded.astype(jnp.float32)

    def rows_of(q, i):
        start = q * block + i * SUB
        return start if isinstance(start, int) else pl.multiple_of(start, SUB)

    def pack(q):
        packed = zero
        for i in range(inner):
            start = rows_of(q, i)
            piece = q * inner + i

            def rows_at(z, offset):
                return field[z, pl.ds(SUB + start + offset, SUB), :]

            strips = []
            for z in range(0, dep, 2):
                for other in range(2):
                    j = i * dep + z + other
                    turned = pltpu.roll(rows_at(z + other, 0), (4 * j + HALO) % cols, 1)
                    packed = jnp.where((lane >> 2) == j, turned, packed)
                pair = jnp.concatenate([rows_at(z, 0), rows_at(z + 1, 0)], axis=0)
                parts[piece, z // 2] = pair.astype(jnp.bfloat16)
                strip = jnp.where(row >= 6, rows_at(z, -8), rows_at(z, 8))
                strip = jnp.where((row == 2) | (row == 3), rows_at(z + 1, -4), strip)
                strip = jnp.where((row == 4) | (row == 5), rows_at(z + 1, 4), strip)
                strips.append(strip)
            for k in range(dep // 4):
                pair = jnp.concatenate(strips[2 * k : 2 * k + 2], axis=0)
                parts[piece, dep // 2 + k] = pair.astype(jnp.bfloat16)
        edge[q] = packed
        for i in range(inner):
            rows_out[q * inner + i] = pltpu.roll(packed, -4 * dep * i % cols, 1)

    each(n_blocks, pack)

    copies = [
        pltpu.make_async_remote_copy(
            source, target, halo_send.at[i], halo_recv.at[i], device_id=to, device_id_type=mesh_id
        )
        for i, (source, target, to) in enumerate(
            [
                (field16.at[pl.ds(dep - HALO, HALO)], low_halo, (me + 1, tile)),
                (field16.at[pl.ds(0, HALO)], high_halo, (me - 1, tile)),
                (edge, edge_left, (me, tile + 1)),
                (edge, edge_right, (me, tile - 1)),
            ]
        )
    ]
    can_send = [me < slabs - 1, me > 0, has_right, has_left]
    can_take = [me > 0, me < slabs - 1, has_left, has_right]
    landing = [low_halo, high_halo, edge_left, edge_right]

    def part_copy(other, slot):
        return pltpu.make_async_remote_copy(
            parts.at[other],
            parts_in.at[slot],
            part_send.at[other],
            part_recv.at[slot],
            device_id=(other, tile),
            device_id_type=mesh_id,
        )

    def row_copy(other, slot, to_right, to):
        target, send, recv = (
            (rows_left, left_send, left_recv) if to_right else (rows_right, right_send, right_recv)
        )
        return pltpu.make_async_remote_copy(
            rows_out.at[other],
            target.at[slot],
            send.at[other],
            recv.at[slot],
            device_id=(other, to),
            device_id_type=mesh_id,
        )

    others = [lax.rem(me + k, slabs) for k in range(1, slabs)]
    pl.semaphore_wait(
        barrier,
        slabs - 1 + slabs * (has_left.astype(jnp.int32) + has_right.astype(jnp.int32)),
    )
    for copy, allowed in zip(copies, can_send):
        pl.when(allowed)(copy.start)
    for other in others:
        part_copy(other, me).start()
    for to_right, allowed, to in ((True, has_right, tile + 1), (False, has_left, tile - 1)):

        @pl.when(allowed)
        def _():
            for p in [me] + others:
                row_copy(p, me, to_right, to).start()

    for target, allowed in zip(
        landing + [rows_left, rows_right], can_take + [has_left, has_right]
    ):

        @pl.when(jnp.logical_not(allowed))
        def _():
            target[...] = jnp.zeros(target.shape, target.dtype)

    parts_in[me] = parts[me]
    for load in loads[3:]:
        load.wait()
    ascending = rank[0] < rank[slabs - 1]
    azimuth = jnp.full((SUB, cols), angles[0], jnp.float32)
    elevation = jnp.full((SUB, cols), angles[1], jnp.float32)
    light_z = jnp.sin(elevation)
    light_y = jnp.cos(elevation) * jnp.sin(azimuth)
    light_x = jnp.cos(elevation) * jnp.cos(azimuth)
    at_edge = (lane < HALO) | (lane >= cols - HALO)

    def shading(gz, gy, gx):
        along = light_z * gz + light_y * gy + light_x * gx
        square = gz * gz + gy * gy + gx * gx + 144.0
        return 0.25 + 0.75 * jnp.abs(along) * lax.rsqrt(square)

    def corrected(gx, fix, j):
        return gx + jnp.where(at_edge, pltpu.roll(fix, (cols - HALO - 4 * j) % cols, 1), 0.0)

    for z in range(dep):
        grad_x[z] = matmul(field16[z], stencil)

    def halo_free(q):
        for i in range(inner):
            start = rows_of(q, i)
            here = pl.ds(start, SUB)
            value = [field[z, pl.ds(SUB + start, SUB), :] for z in range(dep)]
            for z in range(dep):

                def at(dy):
                    return field[z, pl.ds(SUB + start + dy, SUB), :]

                grad_y[z, here, :] = (at(-2) - at(2)) + 8.0 * (at(1) - at(-1))
                part = zero
                for dz, factor in ((-2, 1.0), (-1, -8.0), (1, 8.0), (2, -1.0)):
                    if 0 <= z + dz < dep:
                        part = part + factor * value[z + dz]
                grad_z[z, here, :] = part

    each(n_blocks, halo_free)

    for copy, allowed in zip(copies, can_take):
        pl.when(allowed)(copy.wait_recv)

    def finish(q):
        fix = edge_terms(edge_left[q], edge_right[q], lane)
        whole = q * block
        whole = whole if isinstance(whole, int) else pl.multiple_of(whole, block)
        low = [low_halo[z, pl.ds(whole, block), :].astype(jnp.float32) for z in range(HALO)]
        high = [high_halo[z, pl.ds(whole, block), :].astype(jnp.float32) for z in range(HALO)]
        for i in range(inner):
            here = pl.ds(rows_of(q, i), SUB)
            low_i = [v[i * SUB : (i + 1) * SUB] for v in low]
            high_i = [v[i * SUB : (i + 1) * SUB] for v in high]
            shades = []
            for z in range(dep):
                gx = corrected(grad_x[z, here, :], fix, i * dep + z)
                gz = grad_z[z, here, :]
                if z - 2 < 0:
                    gz = gz + low_i[z]
                if z - 1 < 0:
                    gz = gz - 8.0 * low_i[z + 1]
                if z + 1 >= dep:
                    gz = gz + 8.0 * high_i[z + 1 - dep]
                if z + 2 >= dep:
                    gz = gz - high_i[z + 2 - dep]
                shades.append(shading(gz, grad_y[z, here, :], gx))
            shade_sum[0, here, :] = sum(shades) * (1.0 / dep)

    each(n_blocks, finish)

    for other in others:
        part_copy(other, other).wait_recv()
    for to_right, allowed, to in ((True, has_left, tile - 1), (False, has_right, tile + 1)):

        @pl.when(allowed)
        def _():
            for p in [me] + others:
                row_copy(p, p, to_right, to).wait_recv()

    group = min(slabs, inner)
    n_groups = slabs // group

    def unpack(q):
        for i in range(group):
            s = q * group + i
            values = parts_in[s].astype(jnp.float32).reshape(main * 3 // 2, cols)
            for z in range(dep):
                g = HALO + s * dep + z
                first = main + z // 2 * SUB
                strip = values[first : first + SUB]
                if z % 2:
                    strip = pltpu.roll(strip, 4, 0)
                mine[g, pl.ds(0, SUB), :] = strip
                mine[g, pl.ds(SUB, SUB), :] = values[z * SUB : (z + 1) * SUB]
                mine[g, pl.ds(2 * SUB, SUB), :] = strip
        together = parts_in[pl.ds(q * group, group), pl.ds(0, dep // 2)]
        mine_x[pl.ds(q * group, group)] = matmul(
            together.reshape(group * main, cols), stencil
        ).reshape(group, main, cols)

    each(n_groups, unpack)

    def composite(q, carry):
        total, through = list(carry[:3]), carry[3]
        sides = []
        for arrived in (rows_left, rows_right):
            gathered = zero
            for i in range(group):
                turned = pltpu.roll(arrived[q * group + i], 4 * dep * i % cols, 1)
                gathered = jnp.where(lane // (4 * dep) == i, turned, gathered)
            sides.append(gathered)
        fix = edge_terms(*sides, lane)
        for i in range(group):
            s = q * group + i
            visible = rank[s] >= 0
            for z in range(dep):
                g = HALO + s * dep + z

                def at(dz, dy):
                    return mine[g + dz, pl.ds(SUB + dy, SUB), :]

                value = at(0, 0)
                gz = (at(-2, 0) - at(2, 0)) + 8.0 * (at(1, 0) - at(-1, 0))
                gy = (at(0, -2) - at(0, 2)) + 8.0 * (at(0, 1) - at(0, -1))
                gx = corrected(mine_x[s, pl.ds(z * SUB, SUB), :], fix, i * dep + z)
                passed = jnp.exp(-step * (2.0 + 2.0 * jnp.tanh(1.5 * (value - 1.5))))
                passed = jnp.where(visible, passed, 1.0)
                weight = (1.0 - passed) * shading(gz, gy, gx)
                factor_old = jnp.where(ascending, 1.0, passed)
                factor_new = jnp.where(ascending, through, 1.0) * weight
                for k in range(3):
                    colour = 0.5 + 0.5 * jnp.tanh(0.5 * (slope[k] * value + shift[k]))
                    total[k] = total[k] * factor_old + factor_new * colour
                through = through * passed
        return (*total, through)

    start = (zero, zero, zero, zero + 1.0)
    done = composite(0, start) if n_groups == 1 else lax.fori_loop(0, n_groups, composite, start)
    for k in range(3):
        image[k] = done[k]
    image[3] = 1.0 - done[3]

    for copy, allowed in zip(copies, can_send):
        pl.when(allowed)(copy.wait_send)
    for other in others:
        part_copy(other, me).wait_send()
    for to_right, allowed, to in ((True, has_right, tile + 1), (False, has_left, tile - 1)):

        @pl.when(allowed)
        def _():
            for p in [me] + others:
                row_copy(p, me, to_right, to).wait_send()


def store(image, shade, image_out, shade_out, sem):
    copies = [
        pltpu.make_async_copy(image, image_out, sem.at[0]),
        pltpu.make_async_copy(shade, shade_out, sem.at[1]),
    ]
    for copy in copies:
        copy.start()
    for copy in copies:
        copy.wait()


def shards(coarse, residual, levels, slab_rank, light_angles, color_slope, color_shift):
    dep, rows, cols = residual.shape
    slabs, tiles = lax.axis_size("depth"), lax.axis_size("tile")
    row_dev = rows // slabs
    n_chunks = rows // SUB
    n_blocks = n_chunks // min(n_chunks, cols // 4 // dep)
    f32, bf16 = jnp.float32, jnp.bfloat16
    hbm = pl.BlockSpec(memory_space=pltpu.HBM)
    vmem = pl.BlockSpec(memory_space=pltpu.VMEM)
    dma = pltpu.SemaphoreType.DMA
    image, shade = pl.pallas_call(
        functools.partial(kernel, slabs, tiles),
        out_shape=(
            pltpu.VMEM((4, row_dev, cols), f32),
            pltpu.VMEM((1, rows, cols), f32),
        ),
        in_specs=[hbm] * 7,
        out_specs=(vmem, vmem),
        scratch_shapes=[
            pltpu.VMEM(coarse.shape, bf16),
            pltpu.VMEM(residual.shape, bf16),
            pltpu.VMEM(levels.shape, jnp.int32),
            pltpu.SMEM(slab_rank.shape, jnp.int32),
            pltpu.SMEM(light_angles.shape, f32),
            pltpu.SMEM(color_slope.shape, f32),
            pltpu.SMEM(color_shift.shape, f32),
            pltpu.VMEM((dep, rows, cols), bf16),
            pltpu.VMEM((dep, rows + 2 * SUB, cols), f32),
            pltpu.VMEM((HALO, rows, cols), bf16),
            pltpu.VMEM((HALO, rows, cols), bf16),
            pltpu.VMEM((n_blocks, SUB, cols), f32),
            pltpu.VMEM((n_blocks, SUB, cols), f32),
            pltpu.VMEM((n_blocks, SUB, cols), f32),
            pltpu.VMEM((slabs, SUB, cols), f32),
            pltpu.VMEM((slabs, SUB, cols), f32),
            pltpu.VMEM((slabs, SUB, cols), f32),
            pltpu.VMEM((slabs, dep * 3 // 4, 2 * SUB, cols), bf16),
            pltpu.VMEM((slabs, dep * 3 // 4, 2 * SUB, cols), bf16),
            pltpu.VMEM((slabs * dep + 2 * HALO, 4 * SUB, cols), f32),
            pltpu.VMEM((slabs, dep * SUB, cols), f32),
            pltpu.VMEM((dep, rows, cols), f32),
            pltpu.VMEM((dep, rows, cols), f32),
            pltpu.VMEM((dep, rows, cols), f32),
            dma((7,)),
            dma((4,)),
            dma((4,)),
            dma((slabs,)),
            dma((slabs,)),
            dma((slabs,)),
            dma((slabs,)),
            dma((slabs,)),
            dma((slabs,)),
        ],
        compiler_params=pltpu.CompilerParams(
            collective_id=0, has_side_effects=True, vmem_limit_bytes=40 * 1024 * 1024
        ),
    )(
        *[
            pltpu.with_memory_space_constraint(x, pltpu.HBM)
            for x in (coarse, residual, levels, slab_rank, light_angles, color_slope, color_shift)
        ]
    )
    return pl.pallas_call(
        store,
        out_shape=(pltpu.HBM(image.shape, f32), pltpu.HBM(shade.shape, f32)),
        in_specs=[vmem] * 2,
        out_specs=(hbm, hbm),
        scratch_shapes=[dma((2,))],
    )(*[pltpu.with_memory_space_constraint(x, pltpu.VMEM) for x in (image, shade)])


def solution(mesh):
    placed = (
        P("depth", None, "tile"),
        P("depth", None, "tile"),
        P("depth", None, "tile"),
        P(),
        P(),
        P(),
        P(),
    )
    return jax.shard_map(
        shards,
        mesh=mesh,
        in_specs=placed,
        out_specs=(P(None, "depth", "tile"), P("depth", None, "tile")),
        check_vma=False,
    )
```
